512 devices in a mesh: pair: 16 (over z_lo, y), row: 4 (over x), col: 8 (over z_hi, core).
Axes of the slice: x: 4, y: 8, z: 8 (z_hi: 4, z_lo: 2; z = z_hi * 2 + z_lo), core: 2. Of those that a mesh axis runs over, the one named last changes fastest.
Arguments:
- integrals: bfloat16 [12288, 4096], P(('pair', 'col')), may hold values from -0.21875 to 0.21875
- inverse_factor: bfloat16 [4096, 4096], P('row', ('pair', 'col')), may hold values from -4 to 4, as said below
- energies: float32 [12288], P('pair'), may hold values from 0.25 to 8
- frequency: float32 [1], replicated, may hold values from 0.5 to 2
Outputs:
- response: float32 [4096, 4096], P(('row', 'pair'), 'col')
The draws below stay inside these ranges and needn't reach their ends.
Inputs may be any that keep to these rules, and one draw needn't show every extreme that they name: `inverse_factor`: zero above the diagonal; the diagonal lies between 0.5 and 3.
All inputs are finite; a program needn't handle non-finite values.
Results may differ from the reference program's by a relative error of at most 0.0025.
Values may be sent and summed in bfloat16 or wider, within the bound.
A program may use at most 64 MiB of HBM per device.

```python
import math
import jax
import jax.numpy as jnp
from jax import lax

NAUX = 4096
PAIRS = 12288


def draw_inverse_factor(key, part):
    key_lower, key_diag = jax.random.split(jax.random.fold_in(key, 7))
    row_index = lax.broadcasted_iota(jnp.int32, (NAUX, NAUX), 0)
    col_index = lax.broadcasted_iota(jnp.int32, (NAUX, NAUX), 1)
    lower_part = jnp.clip(jax.random.normal(key_lower, (NAUX, NAUX), jnp.float32), -6.0, 6.0)
    diagonal_part = jax.random.uniform(key_diag, (NAUX, NAUX), jnp.float32, 1.0, 2.0)
    row_scale = 0.5 * lax.rsqrt(row_index.astype(jnp.float32) + 1.0)
    values = jnp.where(row_index == col_index, diagonal_part, jnp.where(col_index < row_index, lower_part * row_scale, 0.0))
    return values.astype(jnp.bfloat16)


def with_spikes(drawn, own_key, source, target, shards_of, factor):
    owner, partner = [(jnp.arange(drawn.shape[axis_at]) // (drawn.shape[axis_at] // shards_of)).reshape([-1 if axis == axis_at else 1 for axis in range(drawn.ndim)]) for axis_at in (source, target)]
    chosen = jax.random.permutation(own_key, shards_of)[partner]
    strong = (owner == chosen) | (owner == (partner + shards_of // 2) % shards_of)
    return jnp.where(strong, factor * drawn, drawn)


def levels(own_key, shape, pieces, least, top_value):
    level = 1.0
    for dim, shards_of in pieces:
        steps = jax.random.uniform(jax.random.fold_in(jax.random.fold_in(own_key, 6), dim), (shards_of,), jnp.float32, least / len(pieces), top_value / len(pieces))
        level = level * jnp.repeat(jnp.exp(steps), shape[dim] // shards_of).reshape((-1,) + (1,) * (len(shape) - 1 - dim))
    return level


def heavy_noise(stream_key, dims, scale, reach, pieces, heavy, kind=jnp.bfloat16):
    array = scale * jax.random.normal(stream_key, dims, jnp.float32)
    if pieces:
        array = array * levels(stream_key, dims, pieces, -0.22, 0.18)
    return jnp.clip(with_spikes(array, jax.random.fold_in(stream_key, 3), *heavy), -reach, reach).astype(kind)


def setup_inputs(seed: int = 0) -> dict:
    keys = jax.random.split(jax.random.key(seed), 5)
    return {
        "integrals": heavy_noise(keys[0], (PAIRS, NAUX), (PAIRS ** -0.5), 0.21875, ((0, 128),), (0, 1, 128, 5.5)),
        "inverse_factor": draw_inverse_factor(jax.random.fold_in(keys[4], 71), 0),
        "energies": jnp.clip(jnp.exp(math.log(8.0) - 3.465736 * jax.random.uniform(keys[2], (PAIRS,), jnp.float32) ** levels(keys[2], (PAIRS,), ((0, 16),), -0.2, 0.2)), 0.25, 8.0),
        "frequency": jnp.clip(jnp.exp(jax.random.uniform(keys[3], (1,), jnp.float32, math.log(0.5), math.log(2.0))), 0.5, 2.0),
    }


def reference(integrals, inverse_factor, energies, frequency):
    transformed = lax.dot_general(integrals, inverse_factor, (((1,), (1,)), ((), ())), preferred_element_type=jnp.float32).astype(jnp.bfloat16)
    factor = 2.0 * energies / (energies * energies + frequency[0] * frequency[0])
    scaled = (factor[:, None] * transformed.astype(jnp.float32)).astype(jnp.bfloat16)
    return lax.dot_general(scaled, transformed, (((0,), (0,)), ((), ())), preferred_element_type=jnp.float32)
```

```python
import functools

import jax
import jax.numpy as jnp
from jax import lax
from jax.experimental import pallas as pl
from jax.experimental.pallas import tpu as pltpu
from jax.sharding import PartitionSpec as P

MESH = pl.DeviceIdType.MESH
F32, BF16 = jnp.float32, jnp.bfloat16
LAG = 2
NARROW_TERMS = 2


def rem(a, b):
    return lax.rem(a, jnp.int32(b))


def div(a, b):
    return lax.div(a, jnp.int32(b))


def device(x, y, z, c):
    return {"pair": rem(z, 2) * 8 + y, "row": x, "col": div(z, 2) * 2 + c}


def kernel(
    i_ref, l_ref, e_ref, f_ref, out_ref,
    lbuf, i2, tacc, tr, tc, eall, fcol, r, sb16, sb32, rb16, rb32, res,
    init_s, init_r, i_s, i_r, e_s, e_r,
    a1_s, a1_r, b1_s, b1_r, a2_s, a2_r, b2_s, b2_r,
    z_s, z_r, x_s, c_s, x_r, y_s, y_r, o_s, o_r,
):
    pair, x, col = lax.axis_index("pair"), lax.axis_index("row"), lax.axis_index("col")
    zlo, y = div(pair, 8), rem(pair, 8)
    zhi, c = div(col, 2), rem(col, 2)
    z = zhi * 2 + zlo
    j = jnp.where(c == 0, x, 7 - x)
    sibling = device(x, y, z, 1 - c)
    x_next, x_prev = device(rem(x + 1, 4), y, z, c), device(rem(x + 3, 4), y, z, c)
    y_side = (device(x, rem(y + 1, 8), z, c), device(x, rem(y + 7, 8), z, c))
    z_side = (device(x, y, rem(z + 1, 8), c), device(x, y, rem(z + 7, 8), c))
    z_pair = zhi * 2 + 1 - zlo

    def remote(src, dst, ssem, rsem, dev):
        return pltpu.make_async_remote_copy(
            src_ref=src, dst_ref=dst, send_sem=ssem, recv_sem=rsem,
            device_id=dev, device_id_type=MESH)

    barrier = pltpu.get_barrier_semaphore()
    for k in range(1, 16):
        dx, dz, dc = k // 4, (k // 2) % 2, k % 2
        pl.semaphore_signal(
            barrier, inc=1, device_id_type=MESH,
            device_id=device(rem(x + dx, 4), y, zhi * 2 + rem(zlo + dz, 2), rem(c + dc, 2)))
    z_out = jnp.where(zlo == 1, rem(z + 1, 8), rem(z + 7, 8))
    for dev in (*y_side, device(x, y, z_out, c)):
        pl.semaphore_signal(barrier, inc=1, device_id_type=MESH, device_id=dev)
    pl.semaphore_wait(barrier, 18)

    def need(block, zl, yy):
        return zl * 4 + div(yy, 2) <= block

    def init_copies(t, h, act):
        block = 2 * x + t
        ox = jnp.where(block < 4, block, 7 - block)
        oc = jnp.where(block < 4, 0, 1)
        src = l_ref.at[:, pl.ds(t * 512 + h * 256, 256)]
        dst = lbuf.at[h, zlo, y, zhi, pl.ds(c * 32, 32), :]
        mine = jnp.logical_and(ox == x, oc == c)
        needed = need(block, zlo, y)

        @pl.when(jnp.logical_and(needed, mine))
        def _():
            copy = pltpu.make_async_copy(src, dst, init_r.at[c, h])
            if act == "start":
                copy.start()

        @pl.when(jnp.logical_and(needed, jnp.logical_not(mine)))
        def _():
            copy = remote(src, dst, init_s.at[t, h], init_r.at[c, h], device(ox, y, z, oc))
            if act == "start":
                copy.start()
            else:
                copy.wait_send()

    for t in range(2):
        for h in range(2):
            init_copies(t, h, "start")

    mine_i = i2.at[pl.ds(c * 96, 96), :]
    copy_i = remote(i_ref, mine_i, i_s.at[0], i_r.at[0], sibling)
    copy_i.start()
    keep_i = pltpu.make_async_copy(i_ref, mine_i, i_s.at[1])
    keep_i.start()
    copy_e = remote(e_ref, eall.at[zlo], e_s, e_r, device(x, y, z_pair, c))
    copy_e.start()

    mine_needed = need(j, zlo, y)

    def wait_init(sc):
        @pl.when(mine_needed)
        def _():
            for h in range(2):
                slot = lbuf.at[h, zlo, y, zhi, sc * 32:(sc + 1) * 32, :]
                pltpu.make_async_copy(slot, slot, init_r.at[sc, h]).wait()

    def back(pos, s, d):
        return rem(pos + 8 - s, 8) if d == 0 else rem(pos + s, 8)

    def first(s, d, which, act):
        recv = act == "recv"
        step = s + 1 if recv else s
        sems = (a1_s, a1_r) if which == 0 else (b1_s, b1_r)
        if which == 0:
            o = back(y, step, d)
            ok = need(j, zlo, o)
            part = slice(0, 2) if s < 3 else slice(d, d + 1)
            ref = lbuf.at[part, zlo, o, zhi, 0:32, :]
            dev = y_side[d]
        else:
            o = back(z, step, d)
            ok = need(j, rem(o, 2), y)
            part = slice(0, 2) if s < 3 else slice(d, d + 1)
            ref = lbuf.at[part, rem(o, 2), y, div(o, 2), 32:64, :]
            dev = z_side[d]

        @pl.when(ok)
        def _():
            copy = remote(ref, ref, sems[0].at[d, s], sems[1].at[d, s], dev)
            if act == "start":
                copy.start()
            elif recv:
                copy.wait_recv()
            else:
                copy.wait_send()

    for which in range(2):
        wait_init(which)
        for d in range(2):
            first(0, d, which, "start")
    for s in range(1, 4):
        for which in range(2):
            for d in range(2):
                first(s - 1, d, which, "recv")
                first(s, d, which, "start")
    for which in range(2):
        for d in range(2):
            first(3, d, which, "recv")

    def second(s, d, which, piece, act):
        recv = act == "recv"
        step = s + 1 if recv else s
        if which == 0:
            o = back(z, step, d)
            zl = rem(o, 2)
            ok = zl * 4 + piece <= j
            ref = lbuf.at[d, zl, 2 * piece:2 * piece + 2, div(o, 2), 0:32, :]
            dev, ssem, rsem = z_side[d], a2_s.at[d, s, piece], a2_r.at[d, s, piece]
        else:
            o = back(y, step, d)
            ok = need(j, piece, o)
            ref = lbuf.at[d, piece, o, :, 32:64, :]
            dev, ssem, rsem = y_side[d], b2_s.at[d, s, piece], b2_r.at[d, s, piece]

        @pl.when(ok)
        def _():
            copy = remote(ref, ref, ssem, rsem, dev)
            if act == "start":
                copy.start()
            elif recv:
                copy.wait_recv()
            else:
                copy.wait_send()

    def pieces():
        for piece in range(4):
            for which in range(2):
                if which == 1 and piece > 1:
                    continue
                for d in range(2):
                    yield d, which, piece

    for d, which, piece in pieces():
        second(0, d, which, piece, "start")

    eall[zlo] = e_ref[...]
    copy_e.wait_recv()
    w = f_ref[0]
    for zl in range(2):
        e = eall[zl]
        fac = 2.0 * e / (e * e + w * w)
        for k in range(6):
            fcol[zl, k * 128:(k + 1) * 128, :] = jnp.broadcast_to(fac[k:k + 1, :], (128, 128)).T
    tacc[...] = jnp.zeros_like(tacc)
    r[...] = jnp.zeros_like(r)
    copy_i.wait_recv()
    keep_i.wait()

    @pl.loop(1, 7)
    def _(s):
        for d, which, piece in pieces():
            second(s - 1, d, which, piece, "recv")
            second(s, d, which, piece, "start")

    for d, which, piece in pieces():
        second(6, d, which, piece, "recv")

    @pl.loop(0, j + 1)
    def _(kt):
        left = i2[:, pl.ds(pl.multiple_of(kt * 512, 512), 512)]
        for h in range(2):
            right = lbuf[h, div(kt, 4), pl.ds(2 * rem(kt, 4), 2)].reshape(512, 256)
            tacc[h] += jnp.dot(left, right, preferred_element_type=F32)

    for h in range(2):
        tr[h, zlo, zhi] = tacc[h].astype(BF16)

    xr = jnp.where(z < 4, z, 7 - z)
    cr = jnp.where(z < 4, 0, 1)
    dist = rem(x + 4 - xr, 4)
    is_root = jnp.logical_and(dist == 0, c == cr)
    is_relay = jnp.logical_and(dist != 0, c == cr)

    def slot(buf, k, h):
        o = back(z, k, h)
        return buf.at[h, rem(o, 2), div(o, 2)]

    def z_copy(k, h):
        return remote(slot(tr, k, h), slot(tr, k, h), z_s.at[h, k], z_r.at[h, k], z_side[h])

    def z_wait(k, h):
        ref = slot(tr, k + 1, h)
        return remote(ref, ref, z_s.at[h, k], z_r.at[h, k], z_side[h]).wait_recv()

    def x_copy(src, k, h):
        return remote(slot(src, k, h), slot(tc, k, h), x_s.at[h, k], x_r.at[h, k],
                      x_next if h == 0 else x_prev)

    def c_copy(src, k, h):
        return remote(slot(src, k, h), slot(tc, k, h), c_s.at[h, k], x_r.at[h, k], sibling)

    def x_wait(k, h):
        pltpu.make_async_copy(slot(tc, k, h), slot(tc, k, h), x_r.at[h, k]).wait()

    def onward(h):
        return dist < 3 if h == 0 else dist > 1

    @pl.loop(0, 8 + LAG)
    def _(kk):
        for h in range(2):
            @pl.when(jnp.logical_and(kk >= 1, kk <= 7))
            def _():
                z_wait(kk - 1, h)

            @pl.when(kk <= 6)
            def _():
                z_copy(kk, h).start()

            @pl.when(jnp.logical_and(kk <= 7, is_root))
            def _():
                x_copy(tr, kk, h).start()
                c_copy(tr, kk, h).start()
                pltpu.make_async_copy(slot(tr, kk, h), slot(tc, kk, h), x_r.at[h, kk]).start()

        @pl.when(jnp.logical_and(kk >= LAG, is_relay))
        def _():
            for h in range(2):
                x_wait(kk - LAG, h)

                @pl.when(onward(h))
                def _():
                    x_copy(tc, kk - LAG, h).start()

                c_copy(tc, kk - LAG, h).start()

    @pl.when(jnp.logical_not(is_relay))
    def _():
        @pl.loop(0, 8)
        def _(k):
            for h in range(2):
                x_wait(k, h)

    @pl.loop(0, 4)
    def _(g):
        zl, zp = div(g, 2), 2 * rem(g, 2)
        fac = fcol[zl, pl.ds(pl.multiple_of(zp * 192, 384), 384), :]
        fac = jnp.concatenate([fac, fac], axis=1)
        for h in range(2):
            rows = tr[h, zl, pl.ds(zp, 2)].reshape(384, 256).astype(F32)
            rows = (fac * rows).astype(BF16)
            for v in range(2):
                cols = tc[v, zl, pl.ds(zp, 2)].reshape(384, 256)
                r[h * 256:(h + 1) * 256, v * 256:(v + 1) * 256] += lax.dot_general(
                    rows, cols, (((0,), (0,)), ((), ())), preferred_element_type=F32)

    def bufs(q, s):
        return (sb16, rb16) if s + 1 - q <= NARROW_TERMS else (sb32, rb32)

    def y_copy(d, q, s):
        sb, rb = bufs(q, s)
        return remote(sb.at[d, q, s], rb.at[d, q, s], y_s.at[d, q, s], y_r.at[d, q, s], y_side[d])

    def columns(d, q):
        v = d if q == 0 else 1 - d
        return slice(v * 256, (v + 1) * 256)

    for s in range(4):
        for q in range(2):
            if s < q:
                continue
            for d in range(2):
                dest = rem(y + 4 - s, 8) if d == 0 else rem(y + 4 + s, 8)
                total = r[pl.ds(pl.multiple_of(dest * 64, 64), 64), columns(d, q)]
                if s > q:
                    y_copy(d, q, s - 1).wait_recv()
                    total = total + bufs(q, s - 1)[1][d, q, s - 1].astype(F32)
                sb = bufs(q, s)[0]
                sb[d, q, s] = total.astype(sb.dtype)
                y_copy(d, q, s).start()
    for v in range(2):
        y_copy(v, 0, 3).wait_recv()
        y_copy(1 - v, 1, 3).wait_recv()
        res[:, v * 256:(v + 1) * 256] = (
            r[pl.ds(pl.multiple_of(y * 64, 64), 64), v * 256:(v + 1) * 256]
            + bufs(0, 3)[1][v, 0, 3].astype(F32)
            + bufs(1, 3)[1][1 - v, 1, 3].astype(F32))

    px, pz, pc = div(j, 2), rem(j, 2), zlo
    stays = jnp.logical_and(px == x, jnp.logical_and(pz == zlo, pc == c))
    out_copy = remote(res, out_ref, o_s, o_r, device(px, y, zhi * 2 + pz, pc))

    @pl.when(stays)
    def _():
        copy = pltpu.make_async_copy(res, out_ref, o_s)
        copy.start()
        copy.wait()

    @pl.when(jnp.logical_not(stays))
    def _():
        out_copy.start()

    for t in range(2):
        for h in range(2):
            init_copies(t, h, "wait")
    copy_i.wait_send()
    copy_e.wait_send()
    for which in range(2):
        for d in range(2):
            for s in range(4):
                first(s, d, which, "send")

    @pl.loop(0, 7)
    def _(s):
        for d, which, piece in pieces():
            second(s, d, which, piece, "send")
        for h in range(2):
            z_copy(s, h).wait_send()

    @pl.when(c == cr)
    def _():
        @pl.loop(0, 8)
        def _(k):
            for h in range(2):
                @pl.when(onward(h) | (dist == 0))
                def _():
                    x_copy(tc, k, h).wait_send()

                c_copy(tc, k, h).wait_send()

    for s in range(4):
        for q in range(2):
            if s < q:
                continue
            for d in range(2):
                y_copy(d, q, s).wait_send()

    @pl.when(jnp.logical_not(stays))
    def _():
        out_copy.wait()


def on_device(integrals, inverse_factor, energies, frequency):
    dma = pltpu.SemaphoreType.DMA
    vmem = pltpu.VMEM
    anywhere = pl.BlockSpec(memory_space=pl.ANY)
    return pl.pallas_call(
        kernel,
        out_shape=jax.ShapeDtypeStruct((64, 512), F32),
        in_specs=[
            anywhere,
            anywhere,
            pl.BlockSpec(memory_space=pltpu.VMEM),
            pl.BlockSpec(memory_space=pltpu.SMEM),
        ],
        out_specs=anywhere,
        scratch_shapes=[
            vmem((2, 2, 8, 4, 64, 256), BF16),
            vmem((192, 4096), BF16),
            vmem((2, 192, 256), F32),
            vmem((2, 2, 4, 192, 256), BF16),
            vmem((2, 2, 4, 192, 256), BF16),
            vmem((2, 6, 128), F32),
            vmem((2, 768, 128), F32),
            vmem((512, 512), F32),
            vmem((2, 2, 4, 64, 256), BF16),
            vmem((2, 2, 4, 64, 256), F32),
            vmem((2, 2, 4, 64, 256), BF16),
            vmem((2, 2, 4, 64, 256), F32),
            vmem((64, 512), F32),
            dma((2, 2)), dma((2, 2)), dma((2,)), dma((1,)), dma, dma,
            dma((2, 4)), dma((2, 4)), dma((2, 4)), dma((2, 4)),
            dma((2, 7, 4)), dma((2, 7, 4)), dma((2, 7, 2)), dma((2, 7, 2)),
            dma((2, 7)), dma((2, 7)), dma((2, 8)), dma((2, 8)), dma((2, 8)),
            dma((2, 2, 4)), dma((2, 2, 4)), dma, dma,
        ],
        compiler_params=pltpu.CompilerParams(
            collective_id=0, has_side_effects=True, vmem_limit_bytes=40 * 1024 * 1024),
    )(integrals, inverse_factor.T, energies.reshape(6, 128), frequency)


def solution(mesh):
    return jax.shard_map(
        on_device,
        mesh=mesh,
        in_specs=(P(("pair", "col"), None), P("row", ("pair", "col")), P("pair"), P()),
        out_specs=P(("row", "pair"), "col"),
        check_vma=False,
    )
```

```python
import jax
import jax.numpy as jnp
from jax import lax
from jax.experimental import pallas as pl
from jax.experimental.pallas import tpu as pltpu
from jax.sharding import PartitionSpec as P

MESH = pl.DeviceIdType.MESH
F32, BF16 = jnp.float32, jnp.bfloat16
FAR_FIRST = (4, 3, 5, 2, 6, 1, 7)


def rem(a, b):
    return lax.rem(a, jnp.int32(b))


def div(a, b):
    return lax.div(a, jnp.int32(b))


def device(x, y, z, c):
    return {"pair": rem(z, 2) * 8 + y, "row": x, "col": div(z, 2) * 2 + c}


def kernel(
    i_ref, l_ref, e_ref, f_ref, out_ref,
    lbuf, i2, tacc, tr, tc, eall, fcol, r, sb, rb,
    init_s, init_r, i_s, i_r, e_s, e_r,
    near_s, near_r, far_s, far_r,
    z_s, z_r, x_s, c_s, x_r, o_s, o_r,
):
    pair, x, col = lax.axis_index("pair"), lax.axis_index("row"), lax.axis_index("col")
    zlo, y = div(pair, 8), rem(pair, 8)
    zhi, c = div(col, 2), rem(col, 2)
    z = zhi * 2 + zlo
    j = jnp.where(c == 0, x, 7 - x)
    sibling = device(x, y, z, 1 - c)
    x_side = (device(rem(x + 1, 4), y, z, c), device(rem(x + 3, 4), y, z, c))
    y_side = (device(x, rem(y + 1, 8), z, c), device(x, rem(y + 7, 8), z, c))
    z_side = (device(x, y, rem(z + 1, 8), c), device(x, y, rem(z + 7, 8), c))
    z_pair = zhi * 2 + 1 - zlo
    px, pz, pc = div(j, 2), rem(j, 2), zlo
    stays = jnp.logical_and(px == x, jnp.logical_and(pz == zlo, pc == c))
    here = 2 * x + zlo
    sx, sz = jnp.where(here < 4, here, 7 - here), c
    sc = jnp.where(here < 4, 0, 1)

    def remote(src, dst, ssem, rsem, dev):
        return pltpu.make_async_remote_copy(
            src_ref=src, dst_ref=dst, send_sem=ssem, recv_sem=rsem,
            device_id=dev, device_id_type=MESH)

    keep_i = pltpu.make_async_copy(i_ref, i2.at[pl.ds(c * 96, 96), :], i_s.at[1])
    keep_i.start()

    barrier = pltpu.get_barrier_semaphore()

    def hello(dev):
        pl.semaphore_signal(barrier, inc=1, device_id_type=MESH, device_id=dev)

    for k in FAR_FIRST:
        hello(device(px, rem(y + k, 8), zhi * 2 + pz, pc))
        hello(device(sx, rem(y + k, 8), zhi * 2 + sz, sc))
        hello(device(x, rem(y + k, 8), z, c))
    for k in range(1, 4):
        for zl in range(2):
            hello(device(x, y, rem(zhi + k, 4) * 2 + zl, c))
    for k in range(1, 16):
        dx, dz, dc = k // 4, (k // 2) % 2, k % 2
        hello(device(rem(x + dx, 4), y, zhi * 2 + rem(zlo + dz, 2), rem(c + dc, 2)))
    pl.semaphore_wait(barrier, 21 + 6 + 15)

    def need(zl, yy):
        return zl * 4 + div(yy, 2) <= j

    def init_copies(t, act):
        block = 2 * x + t
        ox = jnp.where(block < 4, block, 7 - block)
        oc = jnp.where(block < 4, 0, 1)
        src = l_ref.at[:, pl.ds(t * 512, 512)]
        dst = lbuf.at[zlo, y, zhi, pl.ds(c * 32, 32), :]
        mine = jnp.logical_and(ox == x, oc == c)
        needed = zlo * 4 + div(y, 2) <= block

        @pl.when(jnp.logical_and(needed, mine))
        def _():
            if act == "start":
                pltpu.make_async_copy(src, dst, init_r.at[c]).start()

        @pl.when(jnp.logical_and(needed, jnp.logical_not(mine)))
        def _():
            copy = remote(src, dst, init_s.at[t], init_r.at[c], device(ox, y, z, oc))
            if act == "start":
                copy.start()
            else:
                copy.wait_send()

    for t in range(2):
        init_copies(t, "start")
    copy_e = remote(e_ref, eall.at[zlo], e_s, e_r, device(x, y, z_pair, c))
    copy_e.start()

    mine_needed = need(zlo, y)

    def block(which, zl, yy, zh):
        return lbuf.at[zl, yy, zh, which * 32:which * 32 + 32, :]

    def near(which, k):
        ref = block(which, zlo, y, zhi)
        dev = device(x, rem(y + k, 8), z, c) if which == 0 else device(x, y, rem(z + k, 8), c)
        return remote(ref, ref, near_s.at[which, k], near_r.at[which, k], dev)

    def near_wait(which, k):
        if which == 0:
            ref, ok = block(0, zlo, rem(y + 8 - k, 8), zhi), need(zlo, rem(y + 8 - k, 8))
        else:
            o = rem(z + 8 - k, 8)
            ref, ok = block(1, rem(o, 2), y, div(o, 2)), need(rem(o, 2), y)

        @pl.when(jnp.logical_and(ok, k != 0))
        def _():
            pltpu.make_async_copy(ref, ref, near_r.at[which, k]).wait()

    @pl.when(mine_needed)
    def _():
        for which in range(2):
            ref = block(which, zlo, y, zhi)
            pltpu.make_async_copy(ref, ref, init_r.at[which]).wait()
            for k in FAR_FIRST:
                near(which, k).start()

    copy_i = remote(i_ref, i2.at[pl.ds(c * 96, 96), :], i_s.at[0], i_r.at[0], sibling)
    copy_i.start()

    def back(pos, s, d):
        return rem(pos + 8 - s, 8) if d == 0 else rem(pos + s, 8)

    def far(s, d, which, piece, act):
        step = s + 1 if act == "recv" else s
        if which == 0:
            o = back(z, step, d)
            ok = rem(o, 2) * 4 + piece <= j
            ref = lbuf.at[rem(o, 2), 2 * piece:2 * piece + 2, div(o, 2), 0:32, :]
            dev = z_side[d]
        else:
            o = back(y, step, d)
            zl, half = piece // 2, piece % 2
            ok = need(zl, o)
            ref = lbuf.at[zl, o, 2 * half:2 * half + 2, 32:64, :]
            dev = y_side[d]

        @pl.when(ok)
        def _():
            copy = remote(
                ref, ref, far_s.at[which, d, s, piece], far_r.at[which, d, s, piece], dev)
            if act == "start":
                copy.start()
            elif act == "recv":
                copy.wait_recv()
            else:
                copy.wait_send()

    for piece in range(4):
        for k in range(2):
            near_wait(0, rem(y + 8 - (2 * piece + k), 8))
        for d in range(2):
            far(0, d, 0, piece, "start")
        zl, half = piece // 2, piece % 2
        for k in range(2):
            near_wait(1, rem(z + 8 - (4 * half + 2 * k + zl), 8))
        for d in range(2):
            far(0, d, 1, piece, "start")

    eall[zlo] = e_ref[...]
    copy_e.wait_recv()
    w = f_ref[0]
    for zl in range(2):
        e = eall[zl]
        fac = 2.0 * e / (e * e + w * w)
        for k in range(6):
            fcol[zl, k * 128:(k + 1) * 128, :] = jnp.broadcast_to(fac[k:k + 1, :], (128, 128)).T
    tacc[...] = jnp.zeros_like(tacc)
    r[...] = jnp.zeros_like(r)

    for s in range(1, 4):
        for piece in range(4):
            for which in range(2):
                for d in range(2):
                    far(s - 1, d, which, piece, "recv")
                    if s < 3 or piece % 2 == d:
                        far(s, d, which, piece, "start")
    copy_i.wait_recv()
    keep_i.wait()
    for piece in range(4):
        for which in range(2):
            far(3, piece % 2, which, piece, "recv")

    @pl.loop(0, j + 1)
    def _(kt):
        left = i2[:, pl.ds(pl.multiple_of(kt * 512, 512), 512)]
        right = lbuf[div(kt, 4), pl.ds(2 * rem(kt, 4), 2)].reshape(512, 512)
        tacc[...] += jnp.dot(left, right, preferred_element_type=F32)

    tr[zlo, zhi] = tacc[...].astype(BF16)

    xr = jnp.where(z < 4, z, 7 - z)
    cr = jnp.where(z < 4, 0, 1)
    dist = rem(x + 4 - xr, 4)
    is_root = jnp.logical_and(dist == 0, c == cr)

    def part(buf, o, p):
        return buf.at[rem(o, 2), div(o, 2), p * 96:(p + 1) * 96, :]

    def z_copy(s, d, p):
        ref = part(tr, back(z, s, d), p)
        return remote(ref, ref, z_s.at[d, s, p], z_r.at[d, s, p], z_side[d])

    def z_wait(s, d, p):
        ref = part(tr, back(z, s + 1, d), p)
        remote(ref, ref, z_s.at[d, s, p], z_r.at[d, s, p], z_side[d]).wait_recv()

    def arrivals(s):
        if s == 0:
            return [(p, z, p) for p in range(2)]
        if s == 4:
            return [(14 + d, back(z, 4, d), d) for d in range(2)]
        return [(4 * s - 2 + 2 * p + d, back(z, s, d), p) for p in range(2) for d in range(2)]

    def root_send(n, o, p):
        for k in range(2):
            remote(part(tr, o, p), part(tc, o, p), x_s.at[k, n], x_r.at[n], x_side[k]).start()
        remote(part(tr, o, p), part(tc, o, p), c_s.at[n], x_r.at[n], sibling).start()
        pltpu.make_async_copy(part(tr, o, p), part(tc, o, p), x_r.at[n]).start()

    def x_wait(n, o, p):
        pltpu.make_async_copy(part(tc, o, p), part(tc, o, p), x_r.at[n]).wait()

    def relay(n, o, p):
        x_wait(n, o, p)

        @pl.when(dist == (1 if p == 0 else 3))
        def _():
            remote(part(tc, o, p), part(tc, o, p), x_s.at[p, n], x_r.at[n], x_side[p]).start()

        remote(part(tc, o, p), part(tc, o, p), c_s.at[n], x_r.at[n], sibling).start()

    for p in range(2):
        for d in range(2):
            z_copy(0, d, p).start()

    for s in range(7):
        if s == 0:
            @pl.when(is_root)
            def _():
                for a in arrivals(0):
                    root_send(*a)
        elif s < 5:
            for n, o, p in arrivals(s):
                d = (n - (4 * s - 2)) % 2 if s < 4 else p
                z_wait(s - 1, d, p)
                if s < 3 or (s == 3 and p == d):
                    z_copy(s, d, p).start()

                @pl.when(is_root)
                def _():
                    root_send(n, o, p)
        if 1 <= s <= 5:
            @pl.when(jnp.logical_and(c == cr, rem(dist, 2) == 1))
            def _():
                for a in arrivals(s - 1):
                    relay(*a)
        if 2 <= s:
            @pl.when(jnp.logical_and(c == cr, dist == 2))
            def _():
                for a in arrivals(s - 2):
                    relay(*a)

    @pl.when(jnp.logical_or(c != cr, is_root))
    def _():
        for s in range(5):
            for a in arrivals(s):
                x_wait(*a)

    @pl.loop(0, 4)
    def _(g):
        zl, zp = div(g, 2), 2 * rem(g, 2)
        fac = fcol[zl, pl.ds(pl.multiple_of(zp * 192, 384), 384), :]
        fac = jnp.concatenate([fac] * 4, axis=1)
        rows = tr[zl, pl.ds(zp, 2)].reshape(384, 512).astype(F32)
        rows = (fac * rows).astype(BF16)
        cols = tc[zl, pl.ds(zp, 2)].reshape(384, 512)
        r[...] += lax.dot_general(
            rows, cols, (((0,), (0,)), ((), ())), preferred_element_type=F32)

    sb[...] = r[...].reshape(8, 64, 512).astype(BF16)

    def out_copy(k):
        to = rem(y + k, 8)
        return remote(
            sb.at[to], rb.at[k], o_s.at[k], o_r.at[k], device(px, to, zhi * 2 + pz, pc))

    for k in FAR_FIRST:
        out_copy(k).start()

    @pl.when(stays)
    def _():
        pltpu.make_async_copy(sb.at[y], rb.at[0], o_r.at[0]).start()

    @pl.when(jnp.logical_not(stays))
    def _():
        out_copy(0).start()

    pltpu.make_async_copy(rb.at[0], rb.at[0], o_r.at[0]).wait()
    total = rb[0].astype(F32)
    for k in (1, 7, 2, 6, 3, 5, 4):
        out_copy(k).wait_recv()
        total = total + rb[k].astype(F32)
    out_ref[...] = total

    for t in range(2):
        init_copies(t, "wait")
    copy_i.wait_send()
    copy_e.wait_send()

    @pl.when(mine_needed)
    def _():
        for which in range(2):
            for k in FAR_FIRST:
                near(which, k).wait_send()

    for s in range(4):
        for piece in range(4):
            for which in range(2):
                for d in range(2):
                    if s < 3 or piece % 2 == d:
                        far(s, d, which, piece, "send")
    for s in range(4):
        for p in range(2):
            for d in range(2):
                if s < 3 or p == d:
                    z_copy(s, d, p).wait_send()

    for s in range(5):
        for n, o, p in arrivals(s):
            ref = part(tc, o, p)
            for k in range(2):
                @pl.when(jnp.logical_or(
                    is_root,
                    jnp.logical_and(c == cr, dist == (1 if k == 0 else 3)) if k == p else False))
                def _():
                    remote(ref, ref, x_s.at[k, n], x_r.at[n], x_side[k]).wait_send()

            @pl.when(c == cr)
            def _():
                remote(ref, ref, c_s.at[n], x_r.at[n], sibling).wait_send()

    for k in FAR_FIRST:
        out_copy(k).wait_send()

    @pl.when(jnp.logical_not(stays))
    def _():
        out_copy(0).wait_send()


def on_device(integrals, inverse_factor, energies, frequency):
    dma = pltpu.SemaphoreType.DMA
    vmem = pltpu.VMEM
    anywhere = pl.BlockSpec(memory_space=pl.ANY)
    return pl.pallas_call(
        kernel,
        out_shape=jax.ShapeDtypeStruct((64, 512), F32),
        in_specs=[
            anywhere,
            anywhere,
            pl.BlockSpec(memory_space=pltpu.VMEM),
            pl.BlockSpec(memory_space=pltpu.SMEM),
        ],
        out_specs=pl.BlockSpec(memory_space=pltpu.VMEM),
        scratch_shapes=[
            vmem((2, 8, 4, 64, 512), BF16),
            vmem((192, 4096), BF16),
            vmem((192, 512), F32),
            vmem((2, 4, 192, 512), BF16),
            vmem((2, 4, 192, 512), BF16),
            vmem((2, 6, 128), F32),
            vmem((2, 768, 128), F32),
            vmem((512, 512), F32),
            vmem((8, 64, 512), BF16),
            vmem((8, 64, 512), BF16),
            dma((2,)), dma((2,)), dma((2,)), dma((1,)), dma, dma,
            dma((2, 8)), dma((2, 8)), dma((2, 2, 4, 4)), dma((2, 2, 4, 4)),
            dma((2, 4, 2)), dma((2, 4, 2)), dma((2, 16)), dma((16,)), dma((16,)),
            dma((8,)), dma((8,)),
        ],
        compiler_params=pltpu.CompilerParams(
            collective_id=0, has_side_effects=True, vmem_limit_bytes=60 * 1024 * 1024),
    )(integrals, inverse_factor.T, energies.reshape(6, 128), frequency)


def solution(mesh):
    return jax.shard_map(
        on_device,
        mesh=mesh,
        in_specs=(P(("pair", "col"), None), P("row", ("pair", "col")), P("pair"), P()),
        out_specs=P(("row", "pair"), "col"),
        check_vma=False,
    )
```

```python
import jax
import jax.numpy as jnp
from jax import lax
from jax.experimental import pallas as pl
from jax.experimental.pallas import tpu as pltpu
from jax.sharding import PartitionSpec as P

MESH = pl.DeviceIdType.MESH
F32, BF16 = jnp.float32, jnp.bfloat16
FAR_FIRST = (4, 3, 5, 2, 6, 1, 7)


def rem(a, b):
    return lax.rem(a, jnp.int32(b))


def div(a, b):
    return lax.div(a, jnp.int32(b))


def device(x, y, z, c):
    return {"pair": rem(z, 2) * 8 + y, "row": x, "col": div(z, 2) * 2 + c}


def kernel(
    i_ref, l_ref, e_ref, f_ref, out_ref,
    lbuf, i2, tacc, tr, tc, eall, fcol, r, sb, rb, mid, half_mid, sb2,
    i_s, i_r, e_s, e_r,
    near_s, near_r, far_s, far_r,
    z_s, z_r, x_s, x2_s, c_s, x_r, m_s, m_r, h_s, h_r, o_s, o_r,
):
    pair, x, col = lax.axis_index("pair"), lax.axis_index("row"), lax.axis_index("col")
    zlo, y = div(pair, 8), rem(pair, 8)
    zhi, c = div(col, 2), rem(col, 2)
    z = zhi * 2 + zlo
    low = jnp.where(x == 3, 0, jnp.where(x == 0, 1, jnp.where(x == 2, 2, 3)))
    j = jnp.where(c == 0, low, 7 - low)

    def owner(block):
        low = jnp.where(block < 4, block, 7 - block)
        ox = jnp.where(low == 0, 3, jnp.where(low == 1, 0, jnp.where(low == 2, 2, 1)))
        return ox, jnp.where(block < 4, 0, 1)

    sibling = device(x, y, z, 1 - c)
    x_side = (device(rem(x + 1, 4), y, z, c), device(rem(x + 3, 4), y, z, c))
    y_side = (device(x, rem(y + 1, 8), z, c), device(x, rem(y + 7, 8), z, c))
    z_side = (device(x, y, rem(z + 1, 8), c), device(x, y, rem(z + 7, 8), c))
    z_pair = zhi * 2 + 1 - zlo
    px, pz, pc = div(j, 2), rem(j, 2), zlo
    stays = jnp.logical_and(px == x, jnp.logical_and(pz == zlo, pc == c))
    (sx, sc), sz = owner(2 * x + zlo), c

    def remote(src, dst, ssem, rsem, dev):
        return pltpu.make_async_remote_copy(
            src_ref=src, dst_ref=dst, send_sem=ssem, recv_sem=rsem,
            device_id=dev, device_id_type=MESH)

    keep_i = pltpu.make_async_copy(i_ref, i2.at[pl.ds(c * 96, 96), :], i_s.at[1])
    keep_i.start()

    barrier = pltpu.get_barrier_semaphore()

    def hello(dev):
        pl.semaphore_signal(barrier, inc=1, device_id_type=MESH, device_id=dev)

    def factor_target(t, k, half):
        ox, oc = owner(2 * x + t)
        across = z_pair if half else z
        return device(
            ox, rem(y + jnp.where(c == 0, k, 0), 8),
            jnp.where(c == 0, across, rem(z + k, 8)), oc)

    def factor_source(which, k, half):
        if which == 0:
            return device(div(j, 2), rem(y + 8 - k, 8), z_pair if half else z, 0)
        return device(div(j, 2), y, rem(z + 8 - k, 8), 1)

    def own_block(t):
        ox, oc = owner(2 * x + t)
        return jnp.logical_and(ox == x, oc == c)

    own_any = jnp.logical_or(own_block(0), own_block(1))
    for k in FAR_FIRST:
        for t in range(2):
            hello(factor_target(t, k, 0))
            hello(factor_source(t, k, 0))

            @pl.when(c == 0)
            def _():
                hello(factor_target(t, k, 1))

        hello(factor_source(0, k, 1))
    for t in range(2):
        @pl.when(jnp.logical_not(own_block(t)))
        def _():
            hello(factor_target(t, 0, 0))

        @pl.when(jnp.logical_or(div(j, 2) != x, c != t))
        def _():
            hello(factor_source(t, 0, 0))
    for k in (6, 2, 7, 1):
        hello(device(px, rem(y + k, 8), zhi * 2 + pz, pc))
        hello(device(sx, rem(y + k, 8), zhi * 2 + sz, sc))
        hello(device(x, rem(y + k, 8), z, c))
    hello(device(x, y, jnp.where(zlo == 1, rem(z + 1, 8), rem(z + 7, 8)), c))
    for k in range(1, 16):
        dx, dz, dc = k // 4, (k // 2) % 2, k % 2
        hello(device(rem(x + dx, 4), y, zhi * 2 + rem(zlo + dz, 2), rem(c + dc, 2)))
    pl.semaphore_wait(
        barrier, 39 + 12 + 1 + 15 + jnp.where(c == 0, 14, 0) - jnp.where(own_any, 2, 0))

    def need(zl, yy):
        return zl * 4 + div(yy, 2) <= j

    def factor_rows(t, k, half, act):
        src = l_ref.at[half * 16:half * 16 + 16, pl.ds(t * 512, 512)]
        dst = lbuf.at[zlo, y, zhi, pl.ds(c * 32 + half * 16, 16), :]
        needed = zlo * 4 + div(y, 2) <= 2 * x + t
        if k == 0:
            mine = jnp.logical_and(own_block(t), jnp.logical_or(half == 0, c == 1))

            @pl.when(jnp.logical_and(needed, mine))
            def _():
                if act == "start":
                    pltpu.make_async_copy(src, dst, near_r.at[c, 0, half]).start()

            needed = jnp.logical_and(needed, jnp.logical_not(mine))

        @pl.when(needed)
        def _():
            copy = remote(
                src, dst, near_s.at[t, k, half], near_r.at[c, k, half], factor_target(t, k, half))
            if act == "start":
                copy.start()
            else:
                copy.wait_send()

    for k in (*FAR_FIRST, 0):
        for t in range(2):
            for half in range(2):
                factor_rows(t, k, half, "start")
    copy_e = remote(e_ref, eall.at[zlo], e_s, e_r, device(x, y, z_pair, c))
    copy_e.start()

    def near_wait(zl, yy, zh, first, k, which, half):
        ref = lbuf.at[zl, yy, zh, pl.ds(first, 16), :]

        @pl.when(need(zl, yy))
        def _():
            pltpu.make_async_copy(ref, ref, near_r.at[which, k, half]).wait()

    def near_wait_y(zl, yy):
        half = jnp.where(zlo == zl, 0, 1)
        near_wait(zl, yy, zhi, half * 16, rem(y + 8 - yy, 8), 0, half)

    def near_wait_z(zl, zh):
        for half in range(2):
            near_wait(zl, y, zh, 32 + 16 * half, rem(z + 8 - (2 * zh + zl), 8), 1, half)

    copy_i = remote(i_ref, i2.at[pl.ds(c * 96, 96), :], i_s.at[0], i_r.at[0], sibling)
    copy_i.start()

    def back(pos, s, d):
        return rem(pos + 8 - s, 8) if d == 0 else rem(pos + s, 8)

    def far(s, d, which, piece, act):
        step = s + 1 if act == "recv" else s
        if which == 0:
            o = back(z, step, d)
            zl, u = piece // 4, piece % 4
            ok = piece <= j
            first = jnp.where(rem(o, 2) == zl, 0, 16)
            ref = lbuf.at[zl, 2 * u:2 * u + 2, div(o, 2), pl.ds(first, 16), :]
            dev = z_side[d]
        else:
            o = back(y, step, d)
            zl, half = piece // 2, piece % 2
            ok = need(zl, o)
            ref = lbuf.at[zl, o, 2 * half:2 * half + 2, 32:64, :]
            dev = y_side[d]

        @pl.when(ok)
        def _():
            copy = remote(
                ref, ref, far_s.at[which, d, s, piece], far_r.at[which, d, s, piece], dev)
            if act == "start":
                copy.start()
            elif act == "recv":
                copy.wait_recv()
            else:
                copy.wait_send()

    def pieces():
        for u in range(4):
            for which, piece in ((0, u), (0, u + 4), (1, u)):
                yield which, piece

    for which, piece in pieces():
        if which == 0:
            for k in range(2):
                near_wait_y(piece // 4, 2 * (piece % 4) + k)
        else:
            for k in range(2):
                near_wait_z(piece // 2, 2 * (piece % 2) + k)
        for d in range(2):
            far(0, d, which, piece, "start")

    eall[zlo] = e_ref[...]
    copy_e.wait_recv()
    w = f_ref[0]
    for zl in range(2):
        e = eall[zl]
        fac = 2.0 * e / (e * e + w * w)
        for k in range(6):
            fcol[zl, k * 128:(k + 1) * 128, :] = jnp.broadcast_to(fac[k:k + 1, :], (128, 128)).T
    tacc[...] = jnp.zeros_like(tacc)
    r[...] = jnp.zeros_like(r)

    for s in range(1, 4):
        for which, piece in pieces():
            for d in range(2):
                far(s - 1, d, which, piece, "recv")
                if s < 3 or piece % 2 == d:
                    far(s, d, which, piece, "start")
    copy_i.wait_recv()
    keep_i.wait()
    for which, piece in pieces():
        far(3, piece % 2, which, piece, "recv")

    @pl.loop(0, j + 1)
    def _(kt):
        left = i2[:, pl.ds(pl.multiple_of(kt * 512, 512), 512)]
        right = lbuf[div(kt, 4), pl.ds(2 * rem(kt, 4), 2)].reshape(512, 512)
        tacc[...] += jnp.dot(left, right, preferred_element_type=F32)

    tr[zlo, zhi] = tacc[...].astype(BF16)

    xr, cr = owner(z)
    dist = rem(x + 4 - xr, 4)
    is_root = jnp.logical_and(dist == 0, c == cr)

    def part(buf, o, p):
        return buf.at[rem(o, 2), div(o, 2), p * 96:(p + 1) * 96, :]

    def small(o, q):
        return tr.at[rem(o, 2), div(o, 2), q * 48:(q + 1) * 48, :]

    def z_copy(s, d, q):
        ref = small(back(z, s, d), q)
        return remote(ref, ref, z_s.at[d, s, q], z_r.at[d, s, q], z_side[d])

    def z_wait(s, d, q):
        ref = small(back(z, s + 1, d), q)
        remote(ref, ref, z_s.at[d, s, q], z_r.at[d, s, q], z_side[d]).wait_recv()

    def arrivals(s):
        if s == 0:
            return [(p, z, p) for p in range(2)]
        if s == 4:
            return [(14 + d, back(z, 4, d), d) for d in range(2)]
        return [(4 * s - 2 + 2 * p + d, back(z, s, d), p) for p in range(2) for d in range(2)]

    def root_send(n, o, p):
        if n >= 14:
            remote(part(tr, o, p), part(tc, o, p), x2_s.at[p], x_r.at[n],
                   device(rem(x + 2, 4), y, z, c)).start()
        for k in range(2):
            remote(part(tr, o, p), part(tc, o, p), x_s.at[k, n], x_r.at[n], x_side[k]).start()
        remote(part(tr, o, p), part(tc, o, p), c_s.at[n], x_r.at[n], sibling).start()
        pltpu.make_async_copy(part(tr, o, p), part(tc, o, p), x_r.at[n]).start()

    def x_wait(n, o, p):
        pltpu.make_async_copy(part(tc, o, p), part(tc, o, p), x_r.at[n]).wait()

    def relay(n, o, p):
        x_wait(n, o, p)
        if n < 14:
            @pl.when(dist == (1 if p == 0 else 3))
            def _():
                remote(part(tc, o, p), part(tc, o, p), x_s.at[p, n], x_r.at[n], x_side[p]).start()

        remote(part(tc, o, p), part(tc, o, p), c_s.at[n], x_r.at[n], sibling).start()

    def add_chunks(s):
        for o in (z,) if s == 0 else (back(z, s, 0), back(z, s, 1))[:1 if s == 4 else 2]:
            zl, zh = rem(o, 2), div(o, 2)
            fac = fcol[zl, pl.ds(pl.multiple_of(zh * 192, 64), 192), :]
            fac = jnp.concatenate([fac] * 4, axis=1)
            rows = (fac * tr[zl, zh].astype(F32)).astype(BF16)
            product = lax.dot_general(
                rows, tc[zl, zh], (((0,), (0,)), ((), ())), preferred_element_type=F32)
            r[...] += product

    def settle(s):
        @pl.when(jnp.logical_or(c != cr, is_root))
        def _():
            for a in arrivals(s):
                x_wait(*a)

        add_chunks(s)

    for q in range(4):
        for d in range(2):
            z_copy(0, d, q).start()

    copy_i.wait_send()
    copy_e.wait_send()
    for k in range(8):
        for t in range(2):
            for half in range(2):
                factor_rows(t, k, half, "wait")
    for s in range(4):
        for which, piece in pieces():
            for d in range(2):
                if s < 3 or piece % 2 == d:
                    far(s, d, which, piece, "send")

    for s in range(7):
        if s == 0:
            @pl.when(is_root)
            def _():
                for a in arrivals(0):
                    root_send(*a)
        elif s < 5:
            for n, o, p in arrivals(s):
                d = (n - (4 * s - 2)) % 2 if s < 4 else p
                for q in (2 * p, 2 * p + 1):
                    z_wait(s - 1, d, q)
                    if s < 3 or (s == 3 and p == d):
                        z_copy(s, d, q).start()

                @pl.when(is_root)
                def _():
                    root_send(n, o, p)
        if 1 <= s <= 5:
            @pl.when(jnp.logical_and(c == cr, rem(dist, 2) == 1))
            def _():
                for a in arrivals(s - 1):
                    relay(*a)
        if 2 <= s:
            @pl.when(jnp.logical_and(c == cr, dist == 2))
            def _():
                for a in arrivals(s - 2):
                    relay(*a)
        if s == 4:
            settle(0)
            settle(1)
        if s == 5:
            settle(2)
    settle(3)
    settle(4)

    def rows_of(k):
        return r[pl.ds(pl.multiple_of(rem(y + k, 8) * 64, 64), 64), :]

    def mid_copy(d):
        return remote(sb.at[3 if d == 0 else 5], mid.at[d], m_s.at[d], m_r.at[d], y_side[d])

    def half_copy(d):
        return remote(
            sb.at[4, :, d * 256:(d + 1) * 256], half_mid.at[d], h_s.at[d], h_r.at[d],
            device(x, rem(y + (2 if d == 0 else 6), 8), z, c))

    def out_copy(k):
        src = sb2.at[0 if k == 2 else 1] if k in (2, 6) else sb.at[k]
        return remote(
            src, rb.at[k], o_s.at[k], o_r.at[k], device(px, rem(y + k, 8), zhi * 2 + pz, pc))

    sb[4] = rows_of(4).astype(BF16)
    for d in range(2):
        half_copy(d).start()
    for d in range(2):
        sb[3 if d == 0 else 5] = rows_of(3 if d == 0 else 5).astype(BF16)
        mid_copy(d).start()
    for k in (1, 7):
        sb[k] = rows_of(k).astype(BF16)
        out_copy(k).start()
    sb[0] = rows_of(0).astype(BF16)

    @pl.when(stays)
    def _():
        pltpu.make_async_copy(sb.at[0], rb.at[0], o_r.at[0]).start()

    @pl.when(jnp.logical_not(stays))
    def _():
        out_copy(0).start()

    for s in range(4):
        for q in range(4):
            for d in range(2):
                if s < 3 or q // 2 == d:
                    z_copy(s, d, q).wait_send()
    for s in range(5):
        for n, o, p in arrivals(s):
            ref = part(tc, o, p)
            for k in range(2):
                relays = jnp.logical_and(c == cr, dist == (1 if k == 0 else 3))

                @pl.when(jnp.logical_or(is_root, relays) if k == p and n < 14 else is_root)
                def _():
                    remote(ref, ref, x_s.at[k, n], x_r.at[n], x_side[k]).wait_send()

            if n >= 14:
                @pl.when(is_root)
                def _():
                    remote(ref, ref, x2_s.at[p], x_r.at[n], sibling).wait_send()

            @pl.when(c == cr)
            def _():
                remote(ref, ref, c_s.at[n], x_r.at[n], sibling).wait_send()

    for d in range(2):
        half_copy(d).wait_recv()
        mid_copy(d).wait_recv()
        k = 2 if d == 0 else 6
        total = rows_of(k) + mid[d].astype(F32)
        for v in range(2):
            piece = total[:, v * 256:(v + 1) * 256]
            if v == d:
                piece = piece + half_mid[d].astype(F32)
            sb2[d, :, v * 256:(v + 1) * 256] = piece.astype(BF16)
        out_copy(k).start()

    pltpu.make_async_copy(rb.at[0], rb.at[0], o_r.at[0]).wait()
    total = rb[0].astype(F32)
    for k in (1, 7, 2, 6):
        out_copy(k).wait_recv()
        total = total + rb[k].astype(F32)
    out_ref[...] = total

    for d in range(2):
        mid_copy(d).wait_send()
        half_copy(d).wait_send()
    for k in (1, 7, 2, 6):
        out_copy(k).wait_send()

    @pl.when(jnp.logical_not(stays))
    def _():
        out_copy(0).wait_send()


def on_device(integrals, inverse_factor, energies, frequency):
    dma = pltpu.SemaphoreType.DMA
    vmem = pltpu.VMEM
    anywhere = pl.BlockSpec(memory_space=pl.ANY)
    return pl.pallas_call(
        kernel,
        out_shape=jax.ShapeDtypeStruct((64, 512), F32),
        in_specs=[
            anywhere,
            anywhere,
            pl.BlockSpec(memory_space=pltpu.VMEM),
            pl.BlockSpec(memory_space=pltpu.SMEM),
        ],
        out_specs=pl.BlockSpec(memory_space=pltpu.VMEM),
        scratch_shapes=[
            vmem((2, 8, 4, 64, 512), BF16),
            vmem((192, 4096), BF16),
            vmem((192, 512), F32),
            vmem((2, 4, 192, 512), BF16),
            vmem((2, 4, 192, 512), BF16),
            vmem((2, 6, 128), F32),
            vmem((2, 768, 128), F32),
            vmem((512, 512), F32),
            vmem((8, 64, 512), BF16),
            vmem((8, 64, 512), BF16),
            vmem((2, 64, 512), BF16),
            vmem((2, 64, 256), BF16),
            vmem((2, 64, 512), BF16),
            dma((2,)), dma((1,)), dma, dma,
            dma((2, 8, 2)), dma((2, 8, 2)), dma((2, 2, 4, 8)), dma((2, 2, 4, 8)),
            dma((2, 4, 4)), dma((2, 4, 4)), dma((2, 16)), dma((2,)), dma((16,)), dma((16,)),
            dma((2,)), dma((2,)), dma((2,)), dma((2,)), dma((8,)), dma((8,)),
        ],
        compiler_params=pltpu.CompilerParams(
            collective_id=0, has_side_effects=True, vmem_limit_bytes=60 * 1024 * 1024),
    )(integrals, inverse_factor.T, energies.reshape(6, 128), frequency)


def solution(mesh):
    return jax.shard_map(
        on_device,
        mesh=mesh,
        in_specs=(P(("pair", "col"), None), P("row", ("pair", "col")), P("pair"), P()),
        out_specs=P(("row", "pair"), "col"),
        check_vma=False,
    )
```

```python
import jax
import jax.numpy as jnp
from jax import lax
from jax.experimental import pallas as pl
from jax.experimental.pallas import tpu as pltpu
from jax.sharding import PartitionSpec as P

MESH = pl.DeviceIdType.MESH
F32, BF16 = jnp.float32, jnp.bfloat16


def rem(a, b):
    return lax.rem(a, jnp.int32(b))


def div(a, b):
    return lax.div(a, jnp.int32(b))


def device(x, y, z, c):
    return {"pair": rem(z, 2) * 8 + y, "row": x, "col": div(z, 2) * 2 + c}


def kernel(
    i_ref, l_ref, e_ref, f_ref, out_ref,
    lbuf, i2, tacc, tr, tc, eall, fcol, r, sb, rb, mid, half_mid, sb2,
    i_s, i_r, e_s, e_r,
    near_s, near_r, far_s, far_r,
    z_s, z_r, x_s, x2_s, c_s, x_r, m_s, m_r, h_s, h_r, o_s, o_r,
):
    pair, x, col = lax.axis_index("pair"), lax.axis_index("row"), lax.axis_index("col")
    zlo, y = div(pair, 8), rem(pair, 8)
    zhi, c = div(col, 2), rem(col, 2)
    z = zhi * 2 + zlo
    low = jnp.where(x == 3, 0, jnp.where(x == 0, 1, jnp.where(x == 2, 2, 3)))
    j = jnp.where(c == 0, low, 7 - low)

    def owner(block):
        low = jnp.where(block < 4, block, 7 - block)
        ox = jnp.where(low == 0, 3, jnp.where(low == 1, 0, jnp.where(low == 2, 2, 1)))
        return ox, jnp.where(block < 4, 0, 1)

    sibling = device(x, y, z, 1 - c)
    x_side = (device(rem(x + 1, 4), y, z, c), device(rem(x + 3, 4), y, z, c))
    y_side = (device(x, rem(y + 1, 8), z, c), device(x, rem(y + 7, 8), z, c))
    z_side = (device(x, y, rem(z + 1, 8), c), device(x, y, rem(z + 7, 8), c))
    z_pair = zhi * 2 + 1 - zlo
    px, pz, pc = div(j, 2), rem(j, 2), zlo
    stays = jnp.logical_and(px == x, jnp.logical_and(pz == zlo, pc == c))
    (sx, sc), sz = owner(2 * x + zlo), c

    def remote(src, dst, ssem, rsem, dev):
        return pltpu.make_async_remote_copy(
            src_ref=src, dst_ref=dst, send_sem=ssem, recv_sem=rsem,
            device_id=dev, device_id_type=MESH)

    keep_i = pltpu.make_async_copy(i_ref, i2.at[pl.ds(c * 96, 96), :], i_s.at[1])
    keep_i.start()

    def both(a, b):
        return jnp.logical_and(a, b)

    def either(a, b):
        return jnp.logical_or(a, b)

    barrier = pltpu.get_barrier_semaphore()

    def hello(dev):
        pl.semaphore_signal(barrier, inc=1, device_id_type=MESH, device_id=dev)

    def factor_target(t, k):
        ox, oc = owner(2 * x + t)
        return device(
            ox, rem(y + jnp.where(c == 0, k, 0), 8), rem(z + jnp.where(c == 1, k, 0), 8), oc)

    def factor_source(which, k):
        if which == 0:
            return device(div(j, 2), rem(y + 8 - k, 8), z, 0)
        return device(div(j, 2), y, rem(z + 8 - k, 8), 1)

    def own_block(t):
        ox, oc = owner(2 * x + t)
        return both(ox == x, oc == c)

    own_any = either(own_block(0), own_block(1))

    @pl.loop(1, 8)
    def _(k):
        for t in range(2):
            hello(factor_target(t, k))
            hello(factor_source(t, k))

    for t in range(2):
        @pl.when(jnp.logical_not(own_block(t)))
        def _():
            hello(factor_target(t, 0))

        @pl.when(either(div(j, 2) != x, c != t))
        def _():
            hello(factor_source(t, 0))

    for k in (6, 2, 7, 1):
        hello(device(px, rem(y + k, 8), zhi * 2 + pz, pc))
        hello(device(sx, rem(y + k, 8), zhi * 2 + sz, sc))
        hello(device(x, rem(y + k, 8), z, c))

    @pl.when(jnp.logical_not(stays))
    def _():
        hello(device(px, y, zhi * 2 + pz, pc))
        hello(device(sx, y, zhi * 2 + sz, sc))

    x_far = device(rem(x + 2, 4), y, z, c)
    for dev in (*x_side, x_far, sibling, *z_side):
        hello(dev)
    pl.semaphore_wait(
        barrier, 32 + 12 + 6 + jnp.where(stays, 0, 2) - jnp.where(own_any, 2, 0))

    def need(zl, yy):
        return zl * 4 + div(yy, 2) <= j

    def block(which, zl, yy, zh):
        return lbuf.at[zl, yy, zh, which * 32:which * 32 + 32, :]

    def factor_rows(t, k, act):
        src = l_ref.at[:, pl.ds(t * 512, 512)]
        dst = lbuf.at[zlo, y, zhi, pl.ds(c * 32, 32), :]
        needed = zlo * 4 + div(y, 2) <= 2 * x + t
        mine = both(own_block(t), k == 0)
        if act == "start":
            @pl.when(both(needed, mine))
            def _():
                pltpu.make_async_copy(src, dst, near_r.at[c, 0]).start()

        @pl.when(both(needed, jnp.logical_not(mine)))
        def _():
            copy = remote(src, dst, near_s.at[t, k], near_r.at[c, k], factor_target(t, k))
            if act == "start":
                copy.start()
            else:
                copy.wait_send()

    @pl.loop(0, 8)
    def _(i):
        k = rem(i + 2, 8)
        for t in range(2):
            factor_rows(t, k, "start")

    copy_e = remote(e_ref, eall.at[zlo], e_s, e_r, device(x, y, z_pair, c))
    copy_e.start()

    def near_wait(which, zl, yy, zh):
        ref = block(which, zl, yy, zh)
        k = rem(y + 8 - yy, 8) if which == 0 else rem(z + 8 - (2 * zh + zl), 8)

        @pl.when(need(zl, yy))
        def _():
            pltpu.make_async_copy(ref, ref, near_r.at[which, k]).wait()

    copy_i = remote(i_ref, i2.at[pl.ds(c * 96, 96), :], i_s.at[0], i_r.at[0], sibling)
    copy_i.start()

    def back(pos, s, d):
        return rem(pos + 8 - s, 8) if d == 0 else rem(pos + s, 8)

    def far(s, d, which, piece, cond, act):
        step = s + 1 if act == "recv" else s
        if which == 0:
            o = back(z, step, d)
            ok = rem(o, 2) * 4 + piece <= j
            ref = lbuf.at[rem(o, 2), pl.ds(2 * piece, 2), div(o, 2), 0:32, :]
            dev = z_side[d]
        else:
            o = back(y, step, d)
            zl, half = div(piece, 2), rem(piece, 2)
            ok = need(zl, o)
            ref = lbuf.at[zl, o, pl.ds(2 * half, 2), 32:64, :]
            dev = y_side[d]

        @pl.when(both(ok, cond))
        def _():
            copy = remote(
                ref, ref, far_s.at[which, d, s, piece], far_r.at[which, d, s, piece], dev)
            if act == "start":
                copy.start()
            elif act == "recv":
                copy.wait_recv()
            else:
                copy.wait_send()

    def goes(s, d, p):
        return either(s < 3, both(s == 3, p == d))

    @pl.loop(0, 4)
    def _(piece):
        for k in range(2):
            near_wait(0, zlo, 2 * piece + k, zhi)
        for d in range(2):
            far(0, d, 0, piece, True, "start")
        for k in range(2):
            near_wait(1, div(piece, 2), y, 2 * rem(piece, 2) + k)
        for d in range(2):
            far(0, d, 1, piece, True, "start")

    eall[zlo] = e_ref[...]
    copy_e.wait_recv()
    w = f_ref[0]
    for zl in range(2):
        e = eall[zl]
        fac = 2.0 * e / (e * e + w * w)
        for k in range(6):
            fcol[zl, k * 128:(k + 1) * 128, :] = jnp.broadcast_to(fac[k:k + 1, :], (128, 128)).T
    tacc[...] = jnp.zeros_like(tacc)
    r[...] = jnp.zeros_like(r)

    @pl.loop(1, 5)
    def _(s):
        @pl.loop(0, 4)
        def _(piece):
            for which in range(2):
                for d in range(2):
                    far(s - 1, d, which, piece, goes(s - 1, d, rem(piece, 2)), "recv")
                    far(s, d, which, piece, goes(s, d, rem(piece, 2)), "start")

    copy_i.wait_recv()
    keep_i.wait()

    @pl.loop(0, j + 1)
    def _(kt):
        left = i2[:, pl.ds(pl.multiple_of(kt * 512, 512), 512)]
        right = lbuf[div(kt, 4), pl.ds(2 * rem(kt, 4), 2)].reshape(512, 512)
        tacc[...] += jnp.dot(left, right, preferred_element_type=F32)

    tr[zlo, zhi] = tacc[...].astype(BF16)

    xr, cr = owner(z)
    dist = rem(x + 4 - xr, 4)
    is_root = both(dist == 0, c == cr)

    def part(buf, o, p):
        return buf.at[rem(o, 2), div(o, 2), p * 96:(p + 1) * 96, :]

    def small(o, q):
        return tr.at[rem(o, 2), div(o, 2), q * 48:(q + 1) * 48, :]

    def z_copy(s, d, q):
        ref = small(back(z, s, d), q)
        return remote(ref, ref, z_s.at[d, s, q], z_r.at[d, s, q], z_side[d])

    def z_wait(s, d, q):
        ref = small(back(z, s + 1, d), q)
        remote(ref, ref, z_s.at[d, s, q], z_r.at[d, s, q], z_side[d]).wait_recv()

    for q in range(4):
        for d in range(2):
            z_copy(0, d, q).start()

    def arrivals(s, act):
        for p in range(2):
            for d in range(2):
                @pl.when(both(either(s > 0, d == 0), either(s < 4, p == d)))
                def _():
                    act(s, p, d)

    def root_send(s, p, d):
        o, n = back(z, s, d), s * 4 + 2 * p + d

        @pl.when(s == 4)
        def _():
            remote(part(tr, o, p), part(tc, o, p), x2_s.at[p], x_r.at[n], x_far).start()

        for k in range(2):
            remote(part(tr, o, p), part(tc, o, p), x_s.at[k, n], x_r.at[n], x_side[k]).start()
        remote(part(tr, o, p), part(tc, o, p), c_s.at[n], x_r.at[n], sibling).start()
        pltpu.make_async_copy(part(tr, o, p), part(tc, o, p), x_r.at[n]).start()

    def x_wait(s, p, d):
        ref = part(tc, back(z, s, d), p)
        pltpu.make_async_copy(ref, ref, x_r.at[s * 4 + 2 * p + d]).wait()

    def relay(s, p, d):
        x_wait(s, p, d)
        ref, n = part(tc, back(z, s, d), p), s * 4 + 2 * p + d

        @pl.when(both(s < 4, dist == (1 if p == 0 else 3)))
        def _():
            remote(ref, ref, x_s.at[p, n], x_r.at[n], x_side[p]).start()

        remote(ref, ref, c_s.at[n], x_r.at[n], sibling).start()

    def relays(s):
        @pl.when(both(both(c == cr, rem(dist, 2) == 1), both(s >= 1, s <= 5)))
        def _():
            arrivals(s - 1, relay)

        @pl.when(both(both(c == cr, dist == 2), s >= 2))
        def _():
            arrivals(s - 2, relay)

    def add_chunks(first, last):
        @pl.loop(first, last)
        def _(i):
            h = div(i + 1, 2)
            o = jnp.where(rem(i, 2) == 1, rem(z + 8 - h, 8), rem(z + h, 8))
            zl, zh = rem(o, 2), div(o, 2)
            fac = fcol[zl, pl.ds(pl.multiple_of(zh * 192, 64), 192), :]
            fac = jnp.concatenate([fac] * 4, axis=1)
            rows = (fac * tr[zl, zh].astype(F32)).astype(BF16)
            r[...] += lax.dot_general(
                rows, tc[zl, zh], (((0,), (0,)), ((), ())), preferred_element_type=F32)

    def settle(first, last):
        @pl.when(either(c != cr, is_root))
        def _():
            @pl.loop(first, last)
            def _(s):
                arrivals(s, x_wait)

    copy_i.wait_send()
    copy_e.wait_send()

    @pl.loop(0, 8)
    def _(k):
        for t in range(2):
            factor_rows(t, k, "wait")

    @pl.loop(0, 4)
    def _(s):
        @pl.loop(0, 4)
        def _(piece):
            for which in range(2):
                for d in range(2):
                    far(s, d, which, piece, goes(s, d, rem(piece, 2)), "send")

    @pl.when(is_root)
    def _():
        for p in range(2):
            root_send(0, p, 0)

    @pl.loop(1, 5)
    def _(s):
        for p in range(2):
            for d in range(2):
                @pl.when(either(s < 4, p == d))
                def _():
                    for q in (2 * p, 2 * p + 1):
                        z_wait(s - 1, d, q)

                        @pl.when(goes(s, d, p))
                        def _():
                            z_copy(s, d, q).start()

                    @pl.when(is_root)
                    def _():
                        root_send(s, p, d)

        relays(s)

    settle(0, 3)
    add_chunks(0, 5)

    @pl.loop(5, 7)
    def _(s):
        relays(s)

    settle(3, 5)
    add_chunks(5, 8)

    def rows_of(k):
        return r[pl.ds(pl.multiple_of(rem(y + k, 8) * 64, 64), 64), :]

    def mid_copy(d):
        return remote(sb.at[3 if d == 0 else 5], mid.at[d], m_s.at[d], m_r.at[d], y_side[d])

    def half_copy(d):
        return remote(
            sb.at[4, :, d * 256:(d + 1) * 256], half_mid.at[d], h_s.at[d], h_r.at[d],
            device(x, rem(y + (2 if d == 0 else 6), 8), z, c))

    def out_copy(k):
        src = sb2.at[0 if k == 2 else 1] if k in (2, 6) else sb.at[k]
        return remote(
            src, rb.at[k], o_s.at[k], o_r.at[k], device(px, rem(y + k, 8), zhi * 2 + pz, pc))

    sb[4] = rows_of(4).astype(BF16)
    for d in range(2):
        half_copy(d).start()
    for d in range(2):
        sb[3 if d == 0 else 5] = rows_of(3 if d == 0 else 5).astype(BF16)
        mid_copy(d).start()
    for k in (1, 7):
        sb[k] = rows_of(k).astype(BF16)
        out_copy(k).start()
    sb[0] = rows_of(0).astype(BF16)

    @pl.when(stays)
    def _():
        pltpu.make_async_copy(sb.at[0], rb.at[0], o_r.at[0]).start()

    @pl.when(jnp.logical_not(stays))
    def _():
        out_copy(0).start()

    @pl.loop(0, 5)
    def _(s):
        for d in range(2):
            for q in range(4):
                @pl.when(goes(s, d, q // 2))
                def _():
                    z_copy(s, d, q).wait_send()

        def left(s, p, d):
            ref, n = part(tc, back(z, s, d), p), s * 4 + 2 * p + d
            for k in range(2):
                sent = is_root
                if k == p:
                    passed_on = both(both(c == cr, s < 4), dist == (1 if k == 0 else 3))
                    sent = either(is_root, passed_on)

                @pl.when(sent)
                def _():
                    remote(ref, ref, x_s.at[k, n], x_r.at[n], x_side[k]).wait_send()

            @pl.when(both(is_root, s == 4))
            def _():
                remote(ref, ref, x2_s.at[p], x_r.at[n], sibling).wait_send()

            @pl.when(c == cr)
            def _():
                remote(ref, ref, c_s.at[n], x_r.at[n], sibling).wait_send()

        arrivals(s, left)

    for d in range(2):
        half_copy(d).wait_recv()
        mid_copy(d).wait_recv()
        k = 2 if d == 0 else 6
        total = rows_of(k) + mid[d].astype(F32)
        for v in range(2):
            piece = total[:, v * 256:(v + 1) * 256]
            if v == d:
                piece = piece + half_mid[d].astype(F32)
            sb2[d, :, v * 256:(v + 1) * 256] = piece.astype(BF16)
        out_copy(k).start()

    pltpu.make_async_copy(rb.at[0], rb.at[0], o_r.at[0]).wait()
    total = rb[0].astype(F32)
    for k in (1, 7, 2, 6):
        out_copy(k).wait_recv()
        total = total + rb[k].astype(F32)
    out_ref[...] = total

    for d in range(2):
        mid_copy(d).wait_send()
        half_copy(d).wait_send()
    for k in (1, 7, 2, 6):
        out_copy(k).wait_send()

    @pl.when(jnp.logical_not(stays))
    def _():
        out_copy(0).wait_send()


def on_device(integrals, inverse_factor, energies, frequency):
    dma = pltpu.SemaphoreType.DMA
    vmem = pltpu.VMEM
    anywhere = pl.BlockSpec(memory_space=pl.ANY)
    return pl.pallas_call(
        kernel,
        out_shape=jax.ShapeDtypeStruct((64, 512), F32),
        in_specs=[
            anywhere,
            anywhere,
            pl.BlockSpec(memory_space=pltpu.VMEM),
            pl.BlockSpec(memory_space=pltpu.SMEM),
        ],
        out_specs=pl.BlockSpec(memory_space=pltpu.VMEM),
        scratch_shapes=[
            vmem((2, 8, 4, 64, 512), BF16),
            vmem((192, 4096), BF16),
            vmem((192, 512), F32),
            vmem((2, 4, 192, 512), BF16),
            vmem((2, 4, 192, 512), BF16),
            vmem((2, 6, 128), F32),
            vmem((2, 768, 128), F32),
            vmem((512, 512), F32),
            vmem((8, 64, 512), BF16),
            vmem((8, 64, 512), BF16),
            vmem((2, 64, 512), BF16),
            vmem((2, 64, 256), BF16),
            vmem((2, 64, 512), BF16),
            dma((2,)), dma((1,)), dma, dma,
            dma((2, 8)), dma((2, 8)), dma((2, 2, 4, 4)), dma((2, 2, 4, 4)),
            dma((2, 4, 4)), dma((2, 4, 4)), dma((2, 20)), dma((2,)), dma((20,)), dma((20,)),
            dma((2,)), dma((2,)), dma((2,)), dma((2,)), dma((8,)), dma((8,)),
        ],
        compiler_params=pltpu.CompilerParams(
            collective_id=0, has_side_effects=True, vmem_limit_bytes=60 * 1024 * 1024),
    )(integrals, inverse_factor.T, energies.reshape(6, 128), frequency)


def solution(mesh):
    return jax.shard_map(
        on_device,
        mesh=mesh,
        in_specs=(P(("pair", "col"), None), P("row", ("pair", "col")), P("pair"), P()),
        out_specs=P(("row", "pair"), "col"),
        check_vma=False,
    )
```

```python
import jax
import jax.numpy as jnp
from jax import lax
from jax.experimental import pallas as pl
from jax.experimental.pallas import tpu as pltpu
from jax.sharding import PartitionSpec as P

MESH = pl.DeviceIdType.MESH
F32, BF16 = jnp.float32, jnp.bfloat16


def rem(a, b):
    return lax.rem(a, jnp.int32(b))


def div(a, b):
    return lax.div(a, jnp.int32(b))


def device(x, y, z, c):
    return {"pair": rem(z, 2) * 8 + y, "row": x, "col": div(z, 2) * 2 + c}


def kernel(
    i_ref, l_ref, e_ref, f_ref, out_ref,
    lbuf, i2, tacc, tr, tc, eall, fcol, r, sb, rb, mid, half_mid, sb2,
    i_s, i_r, e_s, e_r,
    near_s, near_r, far_s, far_r,
    z_s, z_r, x_s, x2_s, c_s, x_r, m_s, m_r, h_s, h_r, o_s, o_r,
):
    pair, x, col = lax.axis_index("pair"), lax.axis_index("row"), lax.axis_index("col")
    zlo, y = div(pair, 8), rem(pair, 8)
    zhi, c = div(col, 2), rem(col, 2)
    z = zhi * 2 + zlo
    low = jnp.where(x == 3, 0, jnp.where(x == 0, 1, jnp.where(x == 2, 2, 3)))
    j = jnp.where(c == 0, low, 7 - low)

    def owner(block):
        low = jnp.where(block < 4, block, 7 - block)
        ox = jnp.where(low == 0, 3, jnp.where(low == 1, 0, jnp.where(low == 2, 2, 1)))
        return ox, jnp.where(block < 4, 0, 1)

    sibling = device(x, y, z, 1 - c)
    x_side = (device(rem(x + 1, 4), y, z, c), device(rem(x + 3, 4), y, z, c))
    y_side = (device(x, rem(y + 1, 8), z, c), device(x, rem(y + 7, 8), z, c))
    z_side = (device(x, y, rem(z + 1, 8), c), device(x, y, rem(z + 7, 8), c))
    z_pair = zhi * 2 + 1 - zlo
    px, pz, pc = div(j, 2), rem(j, 2), zlo
    stays = jnp.logical_and(px == x, jnp.logical_and(pz == zlo, pc == c))
    (sx, sc), sz = owner(2 * x + zlo), c

    def remote(src, dst, ssem, rsem, dev):
        return pltpu.make_async_remote_copy(
            src_ref=src, dst_ref=dst, send_sem=ssem, recv_sem=rsem,
            device_id=dev, device_id_type=MESH)

    keep_i = pltpu.make_async_copy(i_ref, i2.at[pl.ds(c * 96, 96), :], i_s.at[1])
    keep_i.start()

    def both(a, b):
        return jnp.logical_and(a, b)

    def either(a, b):
        return jnp.logical_or(a, b)

    barrier = pltpu.get_barrier_semaphore()

    def hello(dev):
        pl.semaphore_signal(barrier, inc=1, device_id_type=MESH, device_id=dev)

    def factor_target(t, k):
        ox, oc = owner(2 * x + t)
        return device(
            ox, rem(y + jnp.where(c == 0, k, 0), 8), rem(z + jnp.where(c == 1, k, 0), 8), oc)

    def factor_source(which, k):
        if which == 0:
            return device(div(j, 2), rem(y + 8 - k, 8), z, 0)
        return device(div(j, 2), y, rem(z + 8 - k, 8), 1)

    def own_block(t):
        ox, oc = owner(2 * x + t)
        return both(ox == x, oc == c)

    own_any = either(own_block(0), own_block(1))

    @pl.loop(1, 8)
    def _(k):
        for t in range(2):
            hello(factor_target(t, k))
            hello(factor_source(t, k))

    for t in range(2):
        @pl.when(jnp.logical_not(own_block(t)))
        def _():
            hello(factor_target(t, 0))

        @pl.when(either(div(j, 2) != x, c != t))
        def _():
            hello(factor_source(t, 0))

    for k in (6, 2, 7, 1):
        hello(device(px, rem(y + k, 8), zhi * 2 + pz, pc))
        hello(device(sx, rem(y + k, 8), zhi * 2 + sz, sc))
        hello(device(x, rem(y + k, 8), z, c))

    @pl.when(jnp.logical_not(stays))
    def _():
        hello(device(px, y, zhi * 2 + pz, pc))
        hello(device(sx, y, zhi * 2 + sz, sc))

    x_far = device(rem(x + 2, 4), y, z, c)
    for dev in (*x_side, x_far, sibling, *z_side):
        hello(dev)
    pl.semaphore_wait(
        barrier, 32 + 12 + 6 + jnp.where(stays, 0, 2) - jnp.where(own_any, 2, 0))

    def need(zl, yy):
        return zl * 4 + div(yy, 2) <= j

    def block(which, zl, yy, zh):
        return lbuf.at[zl, yy, zh, which * 32:which * 32 + 32, :]

    def factor_rows(t, k, act):
        src = l_ref.at[:, pl.ds(t * 512, 512)]
        dst = lbuf.at[zlo, y, zhi, pl.ds(c * 32, 32), :]
        needed = zlo * 4 + div(y, 2) <= 2 * x + t
        mine = both(own_block(t), k == 0)
        if act == "start":
            @pl.when(both(needed, mine))
            def _():
                pltpu.make_async_copy(src, dst, near_r.at[c, 0]).start()

        @pl.when(both(needed, jnp.logical_not(mine)))
        def _():
            copy = remote(src, dst, near_s.at[t, k], near_r.at[c, k], factor_target(t, k))
            if act == "start":
                copy.start()
            else:
                copy.wait_send()

    @pl.loop(0, 8)
    def _(i):
        k = rem(i + 2, 8)
        for t in range(2):
            factor_rows(t, k, "start")

    copy_e = remote(e_ref, eall.at[zlo], e_s, e_r, device(x, y, z_pair, c))
    copy_e.start()

    def near_wait(which, zl, yy, zh):
        ref = block(which, zl, yy, zh)
        k = rem(y + 8 - yy, 8) if which == 0 else rem(z + 8 - (2 * zh + zl), 8)

        @pl.when(need(zl, yy))
        def _():
            pltpu.make_async_copy(ref, ref, near_r.at[which, k]).wait()

    copy_i = remote(i_ref, i2.at[pl.ds(c * 96, 96), :], i_s.at[0], i_r.at[0], sibling)
    copy_i.start()

    def back(pos, s, d):
        return rem(pos + 8 - s, 8) if d == 0 else rem(pos + s, 8)

    def far(s, d, which, piece, cond, act):
        step = s + 1 if act == "recv" else s
        if which == 0:
            o = back(z, step, d)
            ok = rem(o, 2) * 4 + piece <= j
            ref = lbuf.at[rem(o, 2), pl.ds(2 * piece, 2), div(o, 2), 0:32, :]
            dev = z_side[d]
        else:
            o = back(y, step, d)
            zl, half = div(piece, 2), rem(piece, 2)
            ok = need(zl, o)
            ref = lbuf.at[zl, o, pl.ds(2 * half, 2), 32:64, :]
            dev = y_side[d]

        @pl.when(both(ok, cond))
        def _():
            copy = remote(
                ref, ref, far_s.at[which, d, s, piece], far_r.at[which, d, s, piece], dev)
            if act == "start":
                copy.start()
            elif act == "recv":
                copy.wait_recv()
            else:
                copy.wait_send()

    def goes(s, d, p):
        return either(s < 3, both(s == 3, p == d))

    @pl.loop(0, 4)
    def _(piece):
        for k in range(2):
            near_wait(0, zlo, 2 * piece + k, zhi)
        for d in range(2):
            far(0, d, 0, piece, True, "start")
        for k in range(2):
            near_wait(1, div(piece, 2), y, 2 * rem(piece, 2) + k)
        for d in range(2):
            far(0, d, 1, piece, True, "start")

    eall[zlo] = e_ref[...]
    copy_e.wait_recv()
    w = f_ref[0]
    for zl in range(2):
        e = eall[zl]
        fac = 2.0 * e / (e * e + w * w)
        for k in range(6):
            fcol[zl, k * 128:(k + 1) * 128, :] = jnp.broadcast_to(fac[k:k + 1, :], (128, 128)).T
    tacc[...] = jnp.zeros_like(tacc)
    r[...] = jnp.zeros_like(r)

    @pl.loop(1, 5)
    def _(s):
        @pl.loop(0, 4)
        def _(piece):
            for which in range(2):
                for d in range(2):
                    far(s - 1, d, which, piece, goes(s - 1, d, rem(piece, 2)), "recv")
                    far(s, d, which, piece, goes(s, d, rem(piece, 2)), "start")

    copy_i.wait_recv()
    keep_i.wait()

    @pl.loop(0, j + 1)
    def _(kt):
        left = i2[:, pl.ds(pl.multiple_of(kt * 512, 512), 512)]
        right = lbuf[div(kt, 4), pl.ds(2 * rem(kt, 4), 2)].reshape(512, 512)
        tacc[...] += jnp.dot(left, right, preferred_element_type=F32)

    tr[zlo, zhi] = tacc[...].astype(BF16)

    xr, cr = owner(z)
    dist = rem(x + 4 - xr, 4)
    is_root = both(dist == 0, c == cr)

    def part(buf, o, p):
        return buf.at[rem(o, 2), div(o, 2), p * 96:(p + 1) * 96, :]

    def small(o, q):
        return tr.at[rem(o, 2), div(o, 2), q * 48:(q + 1) * 48, :]

    def z_copy(s, d, q):
        ref = small(back(z, s, d), q)
        return remote(ref, ref, z_s.at[d, s, q], z_r.at[d, s, q], z_side[d])

    def z_wait(s, d, q):
        ref = small(back(z, s + 1, d), q)
        remote(ref, ref, z_s.at[d, s, q], z_r.at[d, s, q], z_side[d]).wait_recv()

    for q in range(4):
        for d in range(2):
            z_copy(0, d, q).start()

    def arrivals(s, act):
        for p in range(2):
            for d in range(2):
                @pl.when(both(either(s > 0, d == 0), either(s < 4, p == d)))
                def _():
                    act(s, p, d)

    def root_send(s, p, d):
        o, n = back(z, s, d), s * 4 + 2 * p + d

        @pl.when(s == 4)
        def _():
            remote(part(tr, o, p), part(tc, o, p), x2_s.at[p], x_r.at[n], x_far).start()

        for k in range(2):
            remote(part(tr, o, p), part(tc, o, p), x_s.at[k, n], x_r.at[n], x_side[k]).start()
        remote(part(tr, o, p), part(tc, o, p), c_s.at[n], x_r.at[n], sibling).start()
        pltpu.make_async_copy(part(tr, o, p), part(tc, o, p), x_r.at[n]).start()

    def x_wait(s, p, d):
        ref = part(tc, back(z, s, d), p)
        pltpu.make_async_copy(ref, ref, x_r.at[s * 4 + 2 * p + d]).wait()

    def relay(s, p, d):
        x_wait(s, p, d)
        ref, n = part(tc, back(z, s, d), p), s * 4 + 2 * p + d

        @pl.when(both(s < 4, dist == (1 if p == 0 else 3)))
        def _():
            remote(ref, ref, x_s.at[p, n], x_r.at[n], x_side[p]).start()

        remote(ref, ref, c_s.at[n], x_r.at[n], sibling).start()

    def relays(s):
        @pl.when(both(both(c == cr, rem(dist, 2) == 1), both(s >= 1, s <= 5)))
        def _():
            arrivals(s - 1, relay)

        @pl.when(both(both(c == cr, dist == 2), s >= 2))
        def _():
            arrivals(s - 2, relay)

    def add_chunks(first, last):
        @pl.loop(first, last)
        def _(i):
            h = div(i + 1, 2)
            o = jnp.where(rem(i, 2) == 1, rem(z + 8 - h, 8), rem(z + h, 8))
            zl, zh = rem(o, 2), div(o, 2)
            fac = fcol[zl, pl.ds(pl.multiple_of(zh * 192, 64), 192), :]
            fac = jnp.concatenate([fac] * 4, axis=1)
            rows = (fac * tr[zl, zh].astype(F32)).astype(BF16)
            product = lax.dot_general(
                rows, tc[zl, zh], (((0,), (0,)), ((), ())), preferred_element_type=F32)
            r[...] += product

    def settle(first, last):
        @pl.when(either(c != cr, is_root))
        def _():
            @pl.loop(first, last)
            def _(s):
                arrivals(s, x_wait)

    @pl.when(is_root)
    def _():
        for p in range(2):
            root_send(0, p, 0)

    copy_i.wait_send()
    copy_e.wait_send()

    @pl.loop(0, 8)
    def _(k):
        for t in range(2):
            factor_rows(t, k, "wait")

    @pl.loop(0, 4)
    def _(s):
        @pl.loop(0, 4)
        def _(piece):
            for which in range(2):
                for d in range(2):
                    far(s, d, which, piece, goes(s, d, rem(piece, 2)), "send")

    @pl.loop(1, 5)
    def _(s):
        for q in range(4):
            p = q // 2
            for d in range(2):
                @pl.when(either(s < 4, p == d))
                def _():
                    z_wait(s - 1, d, q)

                    @pl.when(goes(s, d, p))
                    def _():
                        z_copy(s, d, q).start()

                    if q % 2:
                        @pl.when(is_root)
                        def _():
                            root_send(s, p, d)

        relays(s)

    settle(0, 3)
    add_chunks(0, 5)

    @pl.loop(5, 7)
    def _(s):
        relays(s)

    settle(3, 5)
    add_chunks(5, 8)

    def rows_of(k):
        return r[pl.ds(pl.multiple_of(rem(y + k, 8) * 64, 64), 64), :]

    def mid_copy(d):
        return remote(sb.at[3 if d == 0 else 5], mid.at[d], m_s.at[d], m_r.at[d], y_side[d])

    def half_copy(d):
        return remote(
            sb.at[4, :, d * 256:(d + 1) * 256], half_mid.at[d], h_s.at[d], h_r.at[d],
            device(x, rem(y + (2 if d == 0 else 6), 8), z, c))

    def out_copy(k):
        src = sb2.at[0 if k == 2 else 1] if k in (2, 6) else sb.at[k]
        return remote(
            src, rb.at[k], o_s.at[k], o_r.at[k], device(px, rem(y + k, 8), zhi * 2 + pz, pc))

    sb[4] = rows_of(4).astype(BF16)
    for d in range(2):
        half_copy(d).start()
    for d in range(2):
        sb[3 if d == 0 else 5] = rows_of(3 if d == 0 else 5).astype(BF16)
        mid_copy(d).start()
    for k in (1, 7):
        sb[k] = rows_of(k).astype(BF16)
        out_copy(k).start()
    sb[0] = rows_of(0).astype(BF16)

    @pl.when(stays)
    def _():
        pltpu.make_async_copy(sb.at[0], rb.at[0], o_r.at[0]).start()

    @pl.when(jnp.logical_not(stays))
    def _():
        out_copy(0).start()

    @pl.loop(0, 5)
    def _(s):
        for d in range(2):
            for q in range(4):
                @pl.when(goes(s, d, q // 2))
                def _():
                    z_copy(s, d, q).wait_send()

        def left(s, p, d):
            ref, n = part(tc, back(z, s, d), p), s * 4 + 2 * p + d
            for k in range(2):
                sent = is_root
                if k == p:
                    passed_on = both(both(c == cr, s < 4), dist == (1 if k == 0 else 3))
                    sent = either(is_root, passed_on)

                @pl.when(sent)
                def _():
                    remote(ref, ref, x_s.at[k, n], x_r.at[n], x_side[k]).wait_send()

            @pl.when(both(is_root, s == 4))
            def _():
                remote(ref, ref, x2_s.at[p], x_r.at[n], sibling).wait_send()

            @pl.when(c == cr)
            def _():
                remote(ref, ref, c_s.at[n], x_r.at[n], sibling).wait_send()

        arrivals(s, left)

    for d in range(2):
        half_copy(d).wait_recv()
        mid_copy(d).wait_recv()
        k = 2 if d == 0 else 6
        total = rows_of(k) + mid[d].astype(F32)
        for v in range(2):
            piece = total[:, v * 256:(v + 1) * 256]
            if v == d:
                piece = piece + half_mid[d].astype(F32)
            sb2[d, :, v * 256:(v + 1) * 256] = piece.astype(BF16)
        out_copy(k).start()

    pltpu.make_async_copy(rb.at[0], rb.at[0], o_r.at[0]).wait()
    total = rb[0].astype(F32)
    for k in (1, 7, 2, 6):
        out_copy(k).wait_recv()
        total = total + rb[k].astype(F32)
    out_ref[...] = total

    for d in range(2):
        mid_copy(d).wait_send()
        half_copy(d).wait_send()
    for k in (1, 7, 2, 6):
        out_copy(k).wait_send()

    @pl.when(jnp.logical_not(stays))
    def _():
        out_copy(0).wait_send()


def on_device(integrals, inverse_factor, energies, frequency):
    dma = pltpu.SemaphoreType.DMA
    vmem = pltpu.VMEM
    in_hbm = pl.BlockSpec(memory_space=pltpu.HBM)
    return pl.pallas_call(
        kernel,
        out_shape=jax.ShapeDtypeStruct((64, 512), F32),
        in_specs=[
            in_hbm,
            in_hbm,
            pl.BlockSpec(memory_space=pltpu.VMEM),
            pl.BlockSpec(memory_space=pltpu.SMEM),
        ],
        out_specs=pl.BlockSpec(memory_space=pltpu.VMEM),
        scratch_shapes=[
            vmem((2, 8, 4, 64, 512), BF16),
            vmem((192, 4096), BF16),
            vmem((192, 512), F32),
            vmem((2, 4, 192, 512), BF16),
            vmem((2, 4, 192, 512), BF16),
            vmem((2, 6, 128), F32),
            vmem((2, 768, 128), F32),
            vmem((512, 512), F32),
            vmem((8, 64, 512), BF16),
            vmem((8, 64, 512), BF16),
            vmem((2, 64, 512), BF16),
            vmem((2, 64, 256), BF16),
            vmem((2, 64, 512), BF16),
            dma((2,)), dma((1,)), dma, dma,
            dma((2, 8)), dma((2, 8)), dma((2, 2, 4, 4)), dma((2, 2, 4, 4)),
            dma((2, 4, 4)), dma((2, 4, 4)), dma((2, 20)), dma((2,)), dma((20,)), dma((20,)),
            dma((2,)), dma((2,)), dma((2,)), dma((2,)), dma((8,)), dma((8,)),
        ],
        compiler_params=pltpu.CompilerParams(
            collective_id=0, has_side_effects=True, vmem_limit_bytes=54528 * 1024),
    )(integrals, inverse_factor.T, energies.reshape(6, 128), frequency)


def solution(mesh):
    return jax.shard_map(
        on_device,
        mesh=mesh,
        in_specs=(P(("pair", "col"), None), P("row", ("pair", "col")), P("pair"), P()),
        out_specs=P(("row", "pair"), "col"),
        check_vma=False,
    )
```

```python
import jax
import jax.numpy as jnp
from jax import lax
from jax.experimental import pallas as pl
from jax.experimental.pallas import tpu as pltpu
from jax.sharding import PartitionSpec as P

MESH = pl.DeviceIdType.MESH
F32, BF16 = jnp.float32, jnp.bfloat16


def rem(a, b):
    return lax.rem(a, jnp.int32(b))


def div(a, b):
    return lax.div(a, jnp.int32(b))


def device(x, y, z, c):
    return {"pair": rem(z, 2) * 8 + y, "row": x, "col": div(z, 2) * 2 + c}


def kernel(
    i_ref, l_ref, e_ref, f_ref, out_ref,
    lbuf, i2, tacc, tr, tc, eall, fcol, r, sb, rb, mid, half_mid, sb2,
    i_s, i_r, e_s, e_r,
    near_s, near_r, far_s, far_r,
    z_s, z_r, x_s, x2_s, c_s, x_r, m_s, m_r, h_s, h_r, o_s, o_r,
):
    pair, x, col = lax.axis_index("pair"), lax.axis_index("row"), lax.axis_index("col")
    zlo, y = div(pair, 8), rem(pair, 8)
    zhi, c = div(col, 2), rem(col, 2)
    z = zhi * 2 + zlo
    low = jnp.where(x == 3, 0, jnp.where(x == 0, 1, jnp.where(x == 2, 2, 3)))
    j = jnp.where(c == 0, low, 7 - low)

    def owner(block):
        low = jnp.where(block < 4, block, 7 - block)
        ox = jnp.where(low == 0, 3, jnp.where(low == 1, 0, jnp.where(low == 2, 2, 1)))
        return ox, jnp.where(block < 4, 0, 1)

    sibling = device(x, y, z, 1 - c)
    x_side = (device(rem(x + 1, 4), y, z, c), device(rem(x + 3, 4), y, z, c))
    y_side = (device(x, rem(y + 1, 8), z, c), device(x, rem(y + 7, 8), z, c))
    z_side = (device(x, y, rem(z + 1, 8), c), device(x, y, rem(z + 7, 8), c))
    z_pair = zhi * 2 + 1 - zlo
    px, pz, pc = div(j, 2), rem(j, 2), zlo
    stays = jnp.logical_and(px == x, jnp.logical_and(pz == zlo, pc == c))
    (sx, sc), sz = owner(2 * x + zlo), c

    def remote(src, dst, ssem, rsem, dev):
        return pltpu.make_async_remote_copy(
            src_ref=src, dst_ref=dst, send_sem=ssem, recv_sem=rsem,
            device_id=dev, device_id_type=MESH)

    keep_i = pltpu.make_async_copy(i_ref, i2.at[pl.ds(c * 96, 96), :], i_s.at[1])
    keep_i.start()

    def both(a, b):
        return jnp.logical_and(a, b)

    def either(a, b):
        return jnp.logical_or(a, b)

    barrier = pltpu.get_barrier_semaphore()

    def hello(dev):
        pl.semaphore_signal(barrier, inc=1, device_id_type=MESH, device_id=dev)

    def crosses(yy):
        return rem(div(yy, 2), 2) == 1

    def factor_target(t, k):
        ox, oc = owner(2 * x + t)
        return device(
            ox, rem(y + jnp.where(c == 0, k, 0), 8),
            jnp.where(c == 0, jnp.where(crosses(y), z_pair, z), rem(z + k, 8)), oc)

    def factor_source(which, k):
        if which == 0:
            from_y = rem(y + 8 - k, 8)
            return device(div(j, 2), from_y, jnp.where(crosses(from_y), z_pair, z), 0)
        return device(div(j, 2), y, rem(z + 8 - k, 8), 1)

    def own_block(t):
        ox, oc = owner(2 * x + t)
        return both(both(ox == x, oc == c), either(c == 1, jnp.logical_not(crosses(y))))

    own_any = either(own_block(0), own_block(1))

    @pl.loop(1, 8)
    def _(k):
        for t in range(2):
            hello(factor_target(t, k))
            hello(factor_source(t, k))

    for t in range(2):
        @pl.when(jnp.logical_not(own_block(t)))
        def _():
            hello(factor_target(t, 0))

        @pl.when(either(either(div(j, 2) != x, c != t), crosses(y) if t == 0 else False))
        def _():
            hello(factor_source(t, 0))

    for k in (6, 2, 7, 1):
        hello(device(px, rem(y + k, 8), zhi * 2 + pz, pc))
        hello(device(sx, rem(y + k, 8), zhi * 2 + sz, sc))
        hello(device(x, rem(y + k, 8), z, c))

    @pl.when(jnp.logical_not(stays))
    def _():
        hello(device(px, y, zhi * 2 + pz, pc))
        hello(device(sx, y, zhi * 2 + sz, sc))

    x_far = device(rem(x + 2, 4), y, z, c)
    for dev in (*x_side, x_far, sibling, *z_side):
        hello(dev)
    pl.semaphore_wait(
        barrier, 32 + 12 + 6 + jnp.where(stays, 0, 2) - jnp.where(own_any, 2, 0))

    def need(zl, yy):
        return zl * 4 + div(yy, 2) <= j

    def block(which, zl, yy, zh):
        return lbuf.at[zl, yy, zh, which * 32:which * 32 + 32, :]

    def factor_rows(t, k, act):
        src = l_ref.at[:, pl.ds(t * 512, 512)]
        dst = lbuf.at[zlo, y, zhi, pl.ds(c * 32, 32), :]
        needed = zlo * 4 + div(y, 2) <= 2 * x + t
        mine = both(own_block(t), k == 0)
        if act == "start":
            @pl.when(both(needed, mine))
            def _():
                pltpu.make_async_copy(src, dst, near_r.at[c, 0]).start()

        @pl.when(both(needed, jnp.logical_not(mine)))
        def _():
            copy = remote(src, dst, near_s.at[t, k], near_r.at[c, k], factor_target(t, k))
            if act == "start":
                copy.start()
            else:
                copy.wait_send()

    @pl.loop(0, 8)
    def _(i):
        k = rem(i + 2, 8)
        for t in range(2):
            factor_rows(t, k, "start")

    copy_e = remote(e_ref, eall.at[zlo], e_s, e_r, device(x, y, z_pair, c))
    copy_e.start()

    def near_wait(which, zl, yy, zh):
        ref = block(which, zl, yy, zh)
        k = rem(y + 8 - yy, 8) if which == 0 else rem(z + 8 - (2 * zh + zl), 8)

        @pl.when(need(zl, yy))
        def _():
            pltpu.make_async_copy(ref, ref, near_r.at[which, k]).wait()

    copy_i = remote(i_ref, i2.at[pl.ds(c * 96, 96), :], i_s.at[0], i_r.at[0], sibling)
    copy_i.start()

    def back(pos, s, d):
        return rem(pos + 8 - s, 8) if d == 0 else rem(pos + s, 8)

    def far(s, d, which, piece, cond, act):
        step = s + 1 if act == "recv" else s
        if which == 0:
            o = back(z, step, d)
            zl = jnp.where(rem(piece, 2) == 0, rem(o, 2), 1 - rem(o, 2))
            ok = zl * 4 + piece <= j
            ref = lbuf.at[zl, pl.ds(2 * piece, 2), div(o, 2), 0:32, :]
            dev = z_side[d]
        else:
            o = back(y, step, d)
            zl, half = div(piece, 2), rem(piece, 2)
            ok = need(zl, o)
            ref = lbuf.at[zl, o, pl.ds(2 * half, 2), 32:64, :]
            dev = y_side[d]

        @pl.when(both(ok, cond))
        def _():
            copy = remote(
                ref, ref, far_s.at[which, d, s, piece], far_r.at[which, d, s, piece], dev)
            if act == "start":
                copy.start()
            elif act == "recv":
                copy.wait_recv()
            else:
                copy.wait_send()

    def goes(s, d, p):
        return either(s < 3, both(s == 3, p == d))

    @pl.loop(0, 4)
    def _(piece):
        for k in range(2):
            near_wait(0, jnp.where(rem(piece, 2) == 0, zlo, 1 - zlo), 2 * piece + k, zhi)
        for d in range(2):
            far(0, d, 0, piece, True, "start")
        for k in range(2):
            near_wait(1, div(piece, 2), y, 2 * rem(piece, 2) + k)
        for d in range(2):
            far(0, d, 1, piece, True, "start")

    eall[zlo] = e_ref[...]
    copy_e.wait_recv()
    w = f_ref[0]
    for zl in range(2):
        e = eall[zl]
        fac = 2.0 * e / (e * e + w * w)
        for k in range(6):
            fcol[zl, k * 128:(k + 1) * 128, :] = jnp.broadcast_to(fac[k:k + 1, :], (128, 128)).T
    tacc[...] = jnp.zeros_like(tacc)
    r[...] = jnp.zeros_like(r)

    @pl.loop(1, 5)
    def _(s):
        @pl.loop(0, 4)
        def _(piece):
            for which in range(2):
                for d in range(2):
                    far(s - 1, d, which, piece, goes(s - 1, d, rem(piece, 2)), "recv")
                    far(s, d, which, piece, goes(s, d, rem(piece, 2)), "start")

    copy_i.wait_recv()
    keep_i.wait()

    @pl.loop(0, j + 1)
    def _(kt):
        left = i2[:, pl.ds(pl.multiple_of(kt * 512, 512), 512)]
        right = lbuf[div(kt, 4), pl.ds(2 * rem(kt, 4), 2)].reshape(512, 512)
        tacc[...] += jnp.dot(left, right, preferred_element_type=F32)

    tr[zlo, zhi] = tacc[...].astype(BF16)

    xr, cr = owner(z)
    dist = rem(x + 4 - xr, 4)
    is_root = both(dist == 0, c == cr)

    def part(buf, o, p):
        return buf.at[rem(o, 2), div(o, 2), p * 96:(p + 1) * 96, :]

    def small(o, q):
        return tr.at[rem(o, 2), div(o, 2), q * 48:(q + 1) * 48, :]

    def z_copy(s, d, q):
        ref = small(back(z, s, d), q)
        return remote(ref, ref, z_s.at[d, s, q], z_r.at[d, s, q], z_side[d])

    def z_wait(s, d, q):
        ref = small(back(z, s + 1, d), q)
        remote(ref, ref, z_s.at[d, s, q], z_r.at[d, s, q], z_side[d]).wait_recv()

    for q in range(4):
        for d in range(2):
            z_copy(0, d, q).start()

    def arrivals(s, act):
        for p in range(2):
            for d in range(2):
                @pl.when(both(either(s > 0, d == 0), either(s < 4, p == d)))
                def _():
                    act(s, p, d)

    def root_send(s, p, d):
        o, n = back(z, s, d), s * 4 + 2 * p + d

        @pl.when(s == 4)
        def _():
            remote(part(tr, o, p), part(tc, o, p), x2_s.at[p], x_r.at[n], x_far).start()

        for k in range(2):
            remote(part(tr, o, p), part(tc, o, p), x_s.at[k, n], x_r.at[n], x_side[k]).start()
        remote(part(tr, o, p), part(tc, o, p), c_s.at[n], x_r.at[n], sibling).start()
        pltpu.make_async_copy(part(tr, o, p), part(tc, o, p), x_r.at[n]).start()

    def x_wait(s, p, d):
        ref = part(tc, back(z, s, d), p)
        pltpu.make_async_copy(ref, ref, x_r.at[s * 4 + 2 * p + d]).wait()

    def relay(s, p, d):
        x_wait(s, p, d)
        ref, n = part(tc, back(z, s, d), p), s * 4 + 2 * p + d

        @pl.when(both(s < 4, dist == (1 if p == 0 else 3)))
        def _():
            remote(ref, ref, x_s.at[p, n], x_r.at[n], x_side[p]).start()

        remote(ref, ref, c_s.at[n], x_r.at[n], sibling).start()

    def relays(s):
        @pl.when(both(both(c == cr, rem(dist, 2) == 1), both(s >= 1, s <= 5)))
        def _():
            arrivals(s - 1, relay)

        @pl.when(both(both(c == cr, dist == 2), s >= 2))
        def _():
            arrivals(s - 2, relay)

    def add_chunks(first, last):
        @pl.loop(first, last)
        def _(i):
            h = div(i + 1, 2)
            o = jnp.where(rem(i, 2) == 1, rem(z + 8 - h, 8), rem(z + h, 8))
            zl, zh = rem(o, 2), div(o, 2)
            fac = fcol[zl, pl.ds(pl.multiple_of(zh * 192, 64), 192), :]
            fac = jnp.concatenate([fac] * 4, axis=1)
            rows = (fac * tr[zl, zh].astype(F32)).astype(BF16)
            product = lax.dot_general(
                rows, tc[zl, zh], (((0,), (0,)), ((), ())), preferred_element_type=F32)
            r[...] += product

    def settle(first, last):
        @pl.when(either(c != cr, is_root))
        def _():
            @pl.loop(first, last)
            def _(s):
                arrivals(s, x_wait)

    @pl.when(is_root)
    def _():
        for p in range(2):
            root_send(0, p, 0)

    copy_i.wait_send()
    copy_e.wait_send()

    @pl.loop(0, 8)
    def _(k):
        for t in range(2):
            factor_rows(t, k, "wait")

    @pl.loop(0, 4)
    def _(s):
        @pl.loop(0, 4)
        def _(piece):
            for which in range(2):
                for d in range(2):
                    far(s, d, which, piece, goes(s, d, rem(piece, 2)), "send")

    @pl.loop(1, 5)
    def _(s):
        for q in range(4):
            p = q // 2
            for d in range(2):
                @pl.when(either(s < 4, p == d))
                def _():
                    z_wait(s - 1, d, q)

                    @pl.when(goes(s, d, p))
                    def _():
                        z_copy(s, d, q).start()

                    if q % 2:
                        @pl.when(is_root)
                        def _():
                            root_send(s, p, d)

        relays(s)

    settle(0, 3)
    add_chunks(0, 5)

    @pl.loop(5, 7)
    def _(s):
        relays(s)

    settle(3, 5)
    add_chunks(5, 8)

    def rows_of(k):
        return r[pl.ds(pl.multiple_of(rem(y + k, 8) * 64, 64), 64), :]

    def mid_copy(d):
        return remote(sb.at[3 if d == 0 else 5], mid.at[d], m_s.at[d], m_r.at[d], y_side[d])

    def half_copy(d):
        return remote(
            sb.at[4, :, d * 256:(d + 1) * 256], half_mid.at[d], h_s.at[d], h_r.at[d],
            device(x, rem(y + (2 if d == 0 else 6), 8), z, c))

    def out_copy(k):
        src = sb2.at[0 if k == 2 else 1] if k in (2, 6) else sb.at[k]
        return remote(
            src, rb.at[k], o_s.at[k], o_r.at[k], device(px, rem(y + k, 8), zhi * 2 + pz, pc))

    sb[4] = rows_of(4).astype(BF16)
    for d in range(2):
        half_copy(d).start()
    for d in range(2):
        sb[3 if d == 0 else 5] = rows_of(3 if d == 0 else 5).astype(BF16)
        mid_copy(d).start()
    for k in (1, 7):
        sb[k] = rows_of(k).astype(BF16)
        out_copy(k).start()
    sb[0] = rows_of(0).astype(BF16)

    @pl.when(stays)
    def _():
        pltpu.make_async_copy(sb.at[0], rb.at[0], o_r.at[0]).start()

    @pl.when(jnp.logical_not(stays))
    def _():
        out_copy(0).start()

    @pl.loop(0, 5)
    def _(s):
        for d in range(2):
            for q in range(4):
                @pl.when(goes(s, d, q // 2))
                def _():
                    z_copy(s, d, q).wait_send()

        def left(s, p, d):
            ref, n = part(tc, back(z, s, d), p), s * 4 + 2 * p + d
            for k in range(2):
                sent = is_root
                if k == p:
                    passed_on = both(both(c == cr, s < 4), dist == (1 if k == 0 else 3))
                    sent = either(is_root, passed_on)

                @pl.when(sent)
                def _():
                    remote(ref, ref, x_s.at[k, n], x_r.at[n], x_side[k]).wait_send()

            @pl.when(both(is_root, s == 4))
            def _():
                remote(ref, ref, x2_s.at[p], x_r.at[n], sibling).wait_send()

            @pl.when(c == cr)
            def _():
                remote(ref, ref, c_s.at[n], x_r.at[n], sibling).wait_send()

        arrivals(s, left)

    for d in range(2):
        half_copy(d).wait_recv()
        mid_copy(d).wait_recv()
        k = 2 if d == 0 else 6
        total = rows_of(k) + mid[d].astype(F32)
        for v in range(2):
            piece = total[:, v * 256:(v + 1) * 256]
            if v == d:
                piece = piece + half_mid[d].astype(F32)
            sb2[d, :, v * 256:(v + 1) * 256] = piece.astype(BF16)
        out_copy(k).start()

    pltpu.make_async_copy(rb.at[0], rb.at[0], o_r.at[0]).wait()
    total = rb[0].astype(F32)
    for k in (1, 7, 2, 6):
        out_copy(k).wait_recv()
        total = total + rb[k].astype(F32)
    out_ref[...] = total

    for d in range(2):
        mid_copy(d).wait_send()
        half_copy(d).wait_send()
    for k in (1, 7, 2, 6):
        out_copy(k).wait_send()

    @pl.when(jnp.logical_not(stays))
    def _():
        out_copy(0).wait_send()


def on_device(integrals, inverse_factor, energies, frequency):
    dma = pltpu.SemaphoreType.DMA
    vmem = pltpu.VMEM
    in_hbm = pl.BlockSpec(memory_space=pltpu.HBM)
    return pl.pallas_call(
        kernel,
        out_shape=jax.ShapeDtypeStruct((64, 512), F32),
        in_specs=[
            in_hbm,
            in_hbm,
            pl.BlockSpec(memory_space=pltpu.VMEM),
            pl.BlockSpec(memory_space=pltpu.SMEM),
        ],
        out_specs=pl.BlockSpec(memory_space=pltpu.VMEM),
        scratch_shapes=[
            vmem((2, 8, 4, 64, 512), BF16),
            vmem((192, 4096), BF16),
            vmem((192, 512), F32),
            vmem((2, 4, 192, 512), BF16),
            vmem((2, 4, 192, 512), BF16),
            vmem((2, 6, 128), F32),
            vmem((2, 768, 128), F32),
            vmem((512, 512), F32),
            vmem((8, 64, 512), BF16),
            vmem((8, 64, 512), BF16),
            vmem((2, 64, 512), BF16),
            vmem((2, 64, 256), BF16),
            vmem((2, 64, 512), BF16),
            dma((2,)), dma((1,)), dma, dma,
            dma((2, 8)), dma((2, 8)), dma((2, 2, 4, 4)), dma((2, 2, 4, 4)),
            dma((2, 4, 4)), dma((2, 4, 4)), dma((2, 20)), dma((2,)), dma((20,)), dma((20,)),
            dma((2,)), dma((2,)), dma((2,)), dma((2,)), dma((8,)), dma((8,)),
        ],
        compiler_params=pltpu.CompilerParams(
            collective_id=0, has_side_effects=True, vmem_limit_bytes=54528 * 1024),
    )(integrals, inverse_factor.T, energies.reshape(6, 128), frequency)


def solution(mesh):
    return jax.shard_map(
        on_device,
        mesh=mesh,
        in_specs=(P(("pair", "col"), None), P("row", ("pair", "col")), P("pair"), P()),
        out_specs=P(("row", "pair"), "col"),
        check_vma=False,
    )
```

```python
import jax
import jax.numpy as jnp
from jax import lax
from jax.experimental import pallas as pl
from jax.experimental.pallas import tpu as pltpu
from jax.sharding import PartitionSpec as P

MESH = pl.DeviceIdType.MESH
F32, BF16 = jnp.float32, jnp.bfloat16


def rem(a, b):
    return lax.rem(a, jnp.int32(b))


def div(a, b):
    return lax.div(a, jnp.int32(b))


def device(x, y, z, c):
    return {"pair": rem(z, 2) * 8 + y, "row": x, "col": div(z, 2) * 2 + c}


def kernel(
    i_ref, l_ref, e_ref, f_ref, out_ref,
    lbuf, i2, tacc, tr, tc, eall, fcol, r, sb, rb, mid, half_mid, sb2,
    i_s, i_r, e_s, e_r,
    near_s, near_r, far_s, far_r,
    z_s, z_r, x_s, x2_s, c_s, x_r, m_s, m_r, h_s, h_r, o_s, o_r,
):
    pair, x, col = lax.axis_index("pair"), lax.axis_index("row"), lax.axis_index("col")
    zlo, y = div(pair, 8), rem(pair, 8)
    zhi, c = div(col, 2), rem(col, 2)
    z = zhi * 2 + zlo
    low = jnp.where(x == 3, 0, jnp.where(x == 0, 1, jnp.where(x == 2, 2, 3)))
    j = jnp.where(c == 0, low, 7 - low)

    def owner(block):
        low = jnp.where(block < 4, block, 7 - block)
        ox = jnp.where(low == 0, 3, jnp.where(low == 1, 0, jnp.where(low == 2, 2, 1)))
        return ox, jnp.where(block < 4, 0, 1)

    sibling = device(x, y, z, 1 - c)
    x_side = (device(rem(x + 1, 4), y, z, c), device(rem(x + 3, 4), y, z, c))
    y_side = (device(x, rem(y + 1, 8), z, c), device(x, rem(y + 7, 8), z, c))
    z_side = (device(x, y, rem(z + 1, 8), c), device(x, y, rem(z + 7, 8), c))
    z_pair = zhi * 2 + 1 - zlo
    px, pz, pc = div(j, 2), rem(j, 2), zlo
    stays = jnp.logical_and(px == x, jnp.logical_and(pz == zlo, pc == c))
    (sx, sc), sz = owner(2 * x + zlo), c

    def remote(src, dst, ssem, rsem, dev):
        return pltpu.make_async_remote_copy(
            src_ref=src, dst_ref=dst, send_sem=ssem, recv_sem=rsem,
            device_id=dev, device_id_type=MESH)

    keep_i = pltpu.make_async_copy(i_ref, i2.at[pl.ds(c * 96, 96), :], i_s.at[1])
    keep_i.start()

    def both(a, b):
        return jnp.logical_and(a, b)

    def either(a, b):
        return jnp.logical_or(a, b)

    barrier = pltpu.get_barrier_semaphore()

    def hello(dev):
        pl.semaphore_signal(barrier, inc=1, device_id_type=MESH, device_id=dev)

    def crosses(yy):
        return rem(div(yy, 2), 2) == 1

    def factor_target(t, k):
        ox, oc = owner(2 * x + t)
        return device(
            ox, rem(y + jnp.where(c == 0, k, 0), 8),
            jnp.where(c == 0, jnp.where(crosses(y), z_pair, z), rem(z + k, 8)), oc)

    def factor_source(which, k):
        if which == 0:
            from_y = rem(y + 8 - k, 8)
            return device(div(j, 2), from_y, jnp.where(crosses(from_y), z_pair, z), 0)
        return device(div(j, 2), y, rem(z + 8 - k, 8), 1)

    def own_block(t):
        ox, oc = owner(2 * x + t)
        return both(both(ox == x, oc == c), either(c == 1, jnp.logical_not(crosses(y))))

    own_any = either(own_block(0), own_block(1))

    @pl.loop(1, 8)
    def _(k):
        for t in range(2):
            hello(factor_target(t, k))
            hello(factor_source(t, k))

    for t in range(2):
        @pl.when(jnp.logical_not(own_block(t)))
        def _():
            hello(factor_target(t, 0))

        @pl.when(either(either(div(j, 2) != x, c != t), crosses(y) if t == 0 else False))
        def _():
            hello(factor_source(t, 0))

    for k in (6, 2, 7, 1):
        hello(device(px, rem(y + k, 8), zhi * 2 + pz, pc))
        hello(device(sx, rem(y + k, 8), zhi * 2 + sz, sc))
        hello(device(x, rem(y + k, 8), z, c))

    @pl.when(jnp.logical_not(stays))
    def _():
        hello(device(px, y, zhi * 2 + pz, pc))
        hello(device(sx, y, zhi * 2 + sz, sc))

    x_far = device(rem(x + 2, 4), y, z, c)
    for dev in (*x_side, x_far, sibling, *z_side):
        hello(dev)
    for k in (2, 6):
        hello(device(x, y, rem(z + k, 8), c))
    pl.semaphore_wait(
        barrier, 32 + 12 + 8 + jnp.where(stays, 0, 2) - jnp.where(own_any, 2, 0))

    def need(zl, yy):
        return zl * 4 + div(yy, 2) <= j

    def block(which, zl, yy, zh):
        return lbuf.at[zl, yy, zh, which * 32:which * 32 + 32, :]

    def factor_rows(t, k, act):
        src = l_ref.at[:, pl.ds(t * 512, 512)]
        dst = lbuf.at[zlo, y, zhi, pl.ds(c * 32, 32), :]
        needed = zlo * 4 + div(y, 2) <= 2 * x + t
        mine = both(own_block(t), k == 0)
        if act == "start":
            @pl.when(both(needed, mine))
            def _():
                pltpu.make_async_copy(src, dst, near_r.at[c, 0]).start()

        @pl.when(both(needed, jnp.logical_not(mine)))
        def _():
            copy = remote(src, dst, near_s.at[t, k], near_r.at[c, k], factor_target(t, k))
            if act == "start":
                copy.start()
            else:
                copy.wait_send()

    @pl.loop(0, 8)
    def _(i):
        k = rem(i + 2, 8)
        for t in range(2):
            factor_rows(t, k, "start")

    copy_e = remote(e_ref, eall.at[zlo], e_s, e_r, device(x, y, z_pair, c))
    copy_e.start()

    def near_wait(which, zl, yy, zh):
        ref = block(which, zl, yy, zh)
        k = rem(y + 8 - yy, 8) if which == 0 else rem(z + 8 - (2 * zh + zl), 8)

        @pl.when(need(zl, yy))
        def _():
            pltpu.make_async_copy(ref, ref, near_r.at[which, k]).wait()

    copy_i = remote(i_ref, i2.at[pl.ds(c * 96, 96), :], i_s.at[0], i_r.at[0], sibling)
    copy_i.start()

    def back(pos, s, d):
        return rem(pos + 8 - s, 8) if d == 0 else rem(pos + s, 8)

    def far(s, d, which, piece, cond, act):
        step = s + 1 if act == "recv" else jnp.where(s == 3, 2, s)
        ahead = jnp.where(s == 3, 2, 1)
        if which == 0:
            o = back(z, step, d)
            zl = jnp.where(rem(piece, 2) == 0, rem(o, 2), 1 - rem(o, 2))
            ok = zl * 4 + piece <= j
            ref = lbuf.at[zl, pl.ds(2 * piece, 2), div(o, 2), 0:32, :]
            dev = device(x, y, back(z, ahead, 1 - d), c)
        else:
            o = back(y, step, d)
            zl, half = div(piece, 2), rem(piece, 2)
            ok = need(zl, o)
            ref = lbuf.at[zl, o, pl.ds(2 * half, 2), 32:64, :]
            dev = device(x, back(y, ahead, 1 - d), z, c)

        @pl.when(both(ok, cond))
        def _():
            copy = remote(
                ref, ref, far_s.at[which, d, s, piece], far_r.at[which, d, s, piece], dev)
            if act == "start":
                copy.start()
            elif act == "recv":
                copy.wait_recv()
            else:
                copy.wait_send()

    def goes(s, d, p):
        return either(s < 3, both(s == 3, p == d))

    @pl.loop(0, 4)
    def _(piece):
        for k in range(2):
            near_wait(0, jnp.where(rem(piece, 2) == 0, zlo, 1 - zlo), 2 * piece + k, zhi)
        for d in range(2):
            far(0, d, 0, piece, True, "start")
        for k in range(2):
            near_wait(1, div(piece, 2), y, 2 * rem(piece, 2) + k)
        for d in range(2):
            far(0, d, 1, piece, True, "start")

    eall[zlo] = e_ref[...]
    copy_e.wait_recv()
    w = f_ref[0]
    for zl in range(2):
        e = eall[zl]
        fac = 2.0 * e / (e * e + w * w)
        for k in range(6):
            fcol[zl, k * 128:(k + 1) * 128, :] = jnp.broadcast_to(fac[k:k + 1, :], (128, 128)).T
    tacc[...] = jnp.zeros_like(tacc)
    r[...] = jnp.zeros_like(r)

    @pl.loop(1, 5)
    def _(s):
        @pl.loop(0, 4)
        def _(piece):
            for which in range(2):
                for d in range(2):
                    far(s - 1, d, which, piece, goes(s - 1, d, rem(piece, 2)), "recv")
                    far(s, d, which, piece, s < 3, "start")
                    far(3, d, which, piece, both(s == 2, d == rem(piece, 2)), "start")

    copy_i.wait_recv()
    keep_i.wait()

    @pl.loop(0, j + 1)
    def _(kt):
        left = i2[:, pl.ds(pl.multiple_of(kt * 512, 512), 512)]
        right = lbuf[div(kt, 4), pl.ds(2 * rem(kt, 4), 2)].reshape(512, 512)
        tacc[...] += jnp.dot(left, right, preferred_element_type=F32)

    tr[zlo, zhi] = tacc[...].astype(BF16)

    xr, cr = owner(z)
    dist = rem(x + 4 - xr, 4)
    is_root = both(dist == 0, c == cr)

    def part(buf, o, p):
        return buf.at[rem(o, 2), div(o, 2), p * 96:(p + 1) * 96, :]

    def small(o, q):
        return tr.at[rem(o, 2), div(o, 2), q * 48:(q + 1) * 48, :]

    def z_copy(s, d, q):
        ref = small(back(z, s, d), q)
        return remote(ref, ref, z_s.at[d, s, q], z_r.at[d, s, q], z_side[d])

    def z_wait(s, d, q):
        ref = small(back(z, s + 1, d), q)
        remote(ref, ref, z_s.at[d, s, q], z_r.at[d, s, q], z_side[d]).wait_recv()

    for q in range(4):
        for d in range(2):
            z_copy(0, d, q).start()

    def arrivals(s, act):
        for p in range(2):
            for d in range(2):
                @pl.when(both(either(s > 0, d == 0), either(s < 4, p == d)))
                def _():
                    act(s, p, d)

    def root_send(s, p, d):
        o, n = back(z, s, d), s * 4 + 2 * p + d

        @pl.when(s == 4)
        def _():
            remote(part(tr, o, p), part(tc, o, p), x2_s.at[p], x_r.at[n], x_far).start()

        for k in range(2):
            remote(part(tr, o, p), part(tc, o, p), x_s.at[k, n], x_r.at[n], x_side[k]).start()
        remote(part(tr, o, p), part(tc, o, p), c_s.at[n], x_r.at[n], sibling).start()
        pltpu.make_async_copy(part(tr, o, p), part(tc, o, p), x_r.at[n]).start()

    def x_wait(s, p, d):
        ref = part(tc, back(z, s, d), p)
        pltpu.make_async_copy(ref, ref, x_r.at[s * 4 + 2 * p + d]).wait()

    def relay(s, p, d):
        x_wait(s, p, d)
        ref, n = part(tc, back(z, s, d), p), s * 4 + 2 * p + d

        @pl.when(both(s < 4, dist == (1 if p == 0 else 3)))
        def _():
            remote(ref, ref, x_s.at[p, n], x_r.at[n], x_side[p]).start()

        remote(ref, ref, c_s.at[n], x_r.at[n], sibling).start()

    def relays(s):
        @pl.when(both(both(c == cr, rem(dist, 2) == 1), both(s >= 1, s <= 5)))
        def _():
            arrivals(s - 1, relay)

        @pl.when(both(both(c == cr, dist == 2), s >= 2))
        def _():
            arrivals(s - 2, relay)

    def add_chunks(first, last):
        @pl.loop(first, last)
        def _(i):
            h = div(i + 1, 2)
            o = jnp.where(rem(i, 2) == 1, rem(z + 8 - h, 8), rem(z + h, 8))
            zl, zh = rem(o, 2), div(o, 2)
            fac = fcol[zl, pl.ds(pl.multiple_of(zh * 192, 64), 192), :]
            fac = jnp.concatenate([fac] * 4, axis=1)
            rows = (fac * tr[zl, zh].astype(F32)).astype(BF16)
            product = lax.dot_general(
                rows, tc[zl, zh], (((0,), (0,)), ((), ())), preferred_element_type=F32)
            r[...] += product

    def settle(first, last):
        @pl.when(either(c != cr, is_root))
        def _():
            @pl.loop(first, last)
            def _(s):
                arrivals(s, x_wait)

    @pl.when(is_root)
    def _():
        for p in range(2):
            root_send(0, p, 0)

    copy_i.wait_send()
    copy_e.wait_send()

    @pl.loop(0, 8)
    def _(k):
        for t in range(2):
            factor_rows(t, k, "wait")

    @pl.loop(0, 4)
    def _(s):
        @pl.loop(0, 4)
        def _(piece):
            for which in range(2):
                for d in range(2):
                    far(s, d, which, piece, goes(s, d, rem(piece, 2)), "send")

    @pl.loop(1, 5)
    def _(s):
        for q in range(4):
            p = q // 2
            for d in range(2):
                @pl.when(either(s < 4, p == d))
                def _():
                    z_wait(s - 1, d, q)

                    @pl.when(goes(s, d, p))
                    def _():
                        z_copy(s, d, q).start()

                    if q % 2:
                        @pl.when(is_root)
                        def _():
                            root_send(s, p, d)

        relays(s)

    settle(0, 3)
    add_chunks(0, 5)

    @pl.loop(5, 7)
    def _(s):
        relays(s)

    settle(3, 5)
    add_chunks(5, 8)

    def rows_of(k):
        return r[pl.ds(pl.multiple_of(rem(y + k, 8) * 64, 64), 64), :]

    def mid_copy(d):
        return remote(sb.at[3 if d == 0 else 5], mid.at[d], m_s.at[d], m_r.at[d], y_side[d])

    def half_copy(d):
        return remote(
            sb.at[4, :, d * 256:(d + 1) * 256], half_mid.at[d], h_s.at[d], h_r.at[d],
            device(x, rem(y + (2 if d == 0 else 6), 8), z, c))

    def out_copy(k):
        src = sb2.at[0 if k == 2 else 1] if k in (2, 6) else sb.at[k]
        return remote(
            src, rb.at[k], o_s.at[k], o_r.at[k], device(px, rem(y + k, 8), zhi * 2 + pz, pc))

    sb[4] = rows_of(4).astype(BF16)
    for d in range(2):
        half_copy(d).start()
    for d in range(2):
        sb[3 if d == 0 else 5] = rows_of(3 if d == 0 else 5).astype(BF16)
        mid_copy(d).start()
    for k in (1, 7):
        sb[k] = rows_of(k).astype(BF16)
        out_copy(k).start()
    sb[0] = rows_of(0).astype(BF16)

    @pl.when(stays)
    def _():
        pltpu.make_async_copy(sb.at[0], rb.at[0], o_r.at[0]).start()

    @pl.when(jnp.logical_not(stays))
    def _():
        out_copy(0).start()

    @pl.loop(0, 5)
    def _(s):
        for d in range(2):
            for q in range(4):
                @pl.when(goes(s, d, q // 2))
                def _():
                    z_copy(s, d, q).wait_send()

        def left(s, p, d):
            ref, n = part(tc, back(z, s, d), p), s * 4 + 2 * p + d
            for k in range(2):
                sent = is_root
                if k == p:
                    passed_on = both(both(c == cr, s < 4), dist == (1 if k == 0 else 3))
                    sent = either(is_root, passed_on)

                @pl.when(sent)
                def _():
                    remote(ref, ref, x_s.at[k, n], x_r.at[n], x_side[k]).wait_send()

            @pl.when(both(is_root, s == 4))
            def _():
                remote(ref, ref, x2_s.at[p], x_r.at[n], sibling).wait_send()

            @pl.when(c == cr)
            def _():
                remote(ref, ref, c_s.at[n], x_r.at[n], sibling).wait_send()

        arrivals(s, left)

    for d in range(2):
        half_copy(d).wait_recv()
        mid_copy(d).wait_recv()
        k = 2 if d == 0 else 6
        total = rows_of(k) + mid[d].astype(F32)
        for v in range(2):
            piece = total[:, v * 256:(v + 1) * 256]
            if v == d:
                piece = piece + half_mid[d].astype(F32)
            sb2[d, :, v * 256:(v + 1) * 256] = piece.astype(BF16)
        out_copy(k).start()

    pltpu.make_async_copy(rb.at[0], rb.at[0], o_r.at[0]).wait()
    total = rb[0].astype(F32)
    for k in (1, 7, 2, 6):
        out_copy(k).wait_recv()
        total = total + rb[k].astype(F32)
    out_ref[...] = total

    for d in range(2):
        mid_copy(d).wait_send()
        half_copy(d).wait_send()
    for k in (1, 7, 2, 6):
        out_copy(k).wait_send()

    @pl.when(jnp.logical_not(stays))
    def _():
        out_copy(0).wait_send()


def on_device(integrals, inverse_factor, energies, frequency):
    dma = pltpu.SemaphoreType.DMA
    vmem = pltpu.VMEM
    in_hbm = pl.BlockSpec(memory_space=pltpu.HBM)
    return pl.pallas_call(
        kernel,
        out_shape=jax.ShapeDtypeStruct((64, 512), F32),
        in_specs=[
            in_hbm,
            in_hbm,
            pl.BlockSpec(memory_space=pltpu.VMEM),
            pl.BlockSpec(memory_space=pltpu.SMEM),
        ],
        out_specs=pl.BlockSpec(memory_space=pltpu.VMEM),
        scratch_shapes=[
            vmem((2, 8, 4, 64, 512), BF16),
            vmem((192, 4096), BF16),
            vmem((192, 512), F32),
            vmem((2, 4, 192, 512), BF16),
            vmem((2, 4, 192, 512), BF16),
            vmem((2, 6, 128), F32),
            vmem((2, 768, 128), F32),
            vmem((512, 512), F32),
            vmem((8, 64, 512), BF16),
            vmem((8, 64, 512), BF16),
            vmem((2, 64, 512), BF16),
            vmem((2, 64, 256), BF16),
            vmem((2, 64, 512), BF16),
            dma((2,)), dma((1,)), dma, dma,
            dma((2, 8)), dma((2, 8)), dma((2, 2, 4, 4)), dma((2, 2, 4, 4)),
            dma((2, 4, 4)), dma((2, 4, 4)), dma((2, 20)), dma((2,)), dma((20,)), dma((20,)),
            dma((2,)), dma((2,)), dma((2,)), dma((2,)), dma((8,)), dma((8,)),
        ],
        compiler_params=pltpu.CompilerParams(
            collective_id=0, has_side_effects=True, vmem_limit_bytes=54528 * 1024),
    )(integrals, inverse_factor.T, energies.reshape(6, 128), frequency)


def solution(mesh):
    return jax.shard_map(
        on_device,
        mesh=mesh,
        in_specs=(P(("pair", "col"), None), P("row", ("pair", "col")), P("pair"), P()),
        out_specs=P(("row", "pair"), "col"),
        check_vma=False,
    )
```
